512 devices in a mesh: corpus: 64 (over x, z), cand: 8 (over y, core).
Axes of the slice: x: 4, y: 4, z: 16, core: 2. Of those that a mesh axis runs over, the one named last changes fastest.
Arguments:
- queries: bfloat16 [65536, 768], P('corpus'), may hold values from -110 to 110
- pool: bfloat16 [65536, 768], P('corpus'), may hold values from -12 to 12
- candidate_block_table: int32 [512, 32], P('corpus', 'cand'), may hold values from 0 to 511, as said below
- pos_slot: int32 [65536], P('corpus'), may hold values from 0 to 31
- pos_row: int32 [65536], P('corpus'), may hold values from 0 to 127
Outputs:
- query_loss: float32 [65536], P('corpus')
- query_gradient_rows: float32 [65536, 768], P(('corpus', 'cand'))
The draws below stay inside these ranges and needn't reach their ends.
Inputs may be any that keep to these rules, and one draw needn't show every extreme that they name: `candidate_block_table`: block ids; block k is held by corpus index k // 8. Among the list slots 4 * c to 4 * c + 3 of the 8 query blocks of one corpus index, no corpus index holds more than 1 of the named blocks (so the 32 blocks a device needs lie on 32 different corpus indices), and at least one corpus index holds exactly 1.
All inputs are finite; a program needn't handle non-finite values.
Results may differ from the reference program's by a relative error of at most 0.0017.
Values may be sent and summed in bfloat16 or wider, within the bound.
No kernel may reach another device: no remote copies, remote signals or barrier semaphores. Data moves between devices by JAX's collectives and lax.ppermute only.
A program may use at most 128 MiB of HBM per device.

```python
import math
import jax
import jax.numpy as jnp
from jax import lax

D = 768
QB = 128
PB = 128
NCD = 4
QBD = 8
PBD = 8
NC = 32
NQB = 512
NQ = 65536
NPB = 512
N_CORPUS = 64
N_CAND = 8


def request_table(key):
    key = jax.random.fold_in(key, 101)
    ask_count = QBD * NCD
    capacity = (2 * ask_count + N_CORPUS - 1) // N_CORPUS
    slot_count = N_CORPUS * capacity

    def one_device(dev_key):
        sub_keys = jax.random.split(dev_key, 4)
        order_score = jax.random.permutation(sub_keys[0], slot_count)
        forced = jax.random.randint(sub_keys[1], (), 0, N_CORPUS)
        slot_ids = jnp.arange(slot_count)
        order_score = jnp.where(slot_ids // capacity == forced, -1 - slot_ids % capacity, order_score)
        chosen = jnp.argsort(order_score)[:ask_count]
        chosen = chosen[jax.random.permutation(sub_keys[2], ask_count)]
        inner_block = jax.random.randint(sub_keys[3], (ask_count,), 0, PBD)
        return (chosen // capacity * PBD + inner_block).astype(jnp.int32)
    device_keys = jax.vmap(lambda device: jax.random.fold_in(key, device))(jnp.arange(N_CORPUS * N_CAND))
    id_table = jax.vmap(one_device)(device_keys)
    id_table = id_table.reshape(N_CORPUS, N_CAND, QBD, NCD).transpose(0, 2, 1, 3)
    return id_table.reshape(N_CORPUS * QBD, N_CAND * NCD)


def positives(key):
    key = jax.random.fold_in(key, 202)
    sub_keys = jax.random.split(key, 2)
    slot_pick = jax.random.randint(sub_keys[0], (NQB * QB,), 0, NC)
    row_pick = jax.random.randint(sub_keys[1], (NQB * QB,), 0, PB)
    return (slot_pick.astype(jnp.int32), row_pick.astype(jnp.int32))


def pool_rows(key, row_ids, pairing):
    key = jax.random.fold_in(key, 303)
    noise_base = jax.random.fold_in(key, 1)
    scale_base = jax.random.fold_in(key, 2)

    def one_row(row_id):
        noise = jax.random.normal(jax.random.fold_in(noise_base, row_id), (D,), jnp.float32)
        shaped = jnp.clip(noise, -4.0, 4.0)
        spread = jnp.exp(jax.random.uniform(jax.random.fold_in(scale_base, row_id // pairing), (), jnp.float32, math.log(0.3), math.log(3.0)))
        return (shaped * spread, spread)
    return jax.vmap(one_row)(row_ids)


def draw_pool(key, part):
    values = pool_rows(key, jnp.arange(NPB * PB), 1)[0]
    return values.astype(jnp.bfloat16)


def draw_candidate_block_table(key, part):
    return request_table(key)


def draw_pos_slot(key, part):
    return positives(key)[0]


def draw_pos_row(key, part):
    return positives(key)[1]


def draw_queries(key, part):
    own_key = jax.random.fold_in(key, 404)
    sub_keys = jax.random.split(own_key, 2)
    count = NQB * QB
    sigma = jnp.exp(jax.random.uniform(sub_keys[0], (count, 1), jnp.float32, math.log(0.3), math.log(3.0)))
    values = jnp.clip(jax.random.normal(sub_keys[1], (count, D), jnp.float32), -4.0, 4.0) * sigma
    return values.astype(jnp.bfloat16)


def setup_inputs(seed: int = 0) -> dict:
    key_list = jax.random.split(jax.random.key(seed), 6)
    return {
        "queries": draw_queries(jax.random.fold_in(key_list[5], 71), 0),
        "pool": draw_pool(jax.random.fold_in(key_list[5], 71), 0),
        "candidate_block_table": draw_candidate_block_table(jax.random.fold_in(key_list[5], 71), 0),
        "pos_slot": draw_pos_slot(jax.random.fold_in(key_list[5], 71), 0),
        "pos_row": draw_pos_row(jax.random.fold_in(key_list[5], 71), 0),
    }


def reference(queries, pool, candidate_block_table, pos_slot, pos_row):
    blocks_all = pool.reshape(NPB, PB, D)
    query_blocks = queries.reshape(NQB, QB, D)
    slots_all = pos_slot.reshape(NQB, QB)
    rows_all = pos_row.reshape(NQB, QB)
    score_scale = D ** -0.5

    def per_block(packed):
        query_rows, block_ids, slot_pick, row_pick = packed
        candidate_row_matrix = blocks_all[block_ids].reshape(NC * PB, D)
        scores = jnp.dot(query_rows, candidate_row_matrix.T, preferred_element_type=jnp.float32) * score_scale
        row_top = jnp.max(scores, axis=1)
        shifted = jnp.exp(scores - row_top[:, None])
        row_total = jnp.sum(shifted, axis=1)
        column = (slot_pick * PB + row_pick).astype(jnp.int32)
        positive = jnp.take_along_axis(scores, column[:, None], axis=1)[:, 0]
        query_loss = row_top + jnp.log(row_total) - positive
        softmax_weight = (shifted / row_total[:, None]).astype(jnp.bfloat16)
        attraction_terms = jnp.dot(softmax_weight, candidate_row_matrix, preferred_element_type=jnp.float32)
        query_gradient_rows = attraction_terms - candidate_row_matrix[column].astype(jnp.float32)
        return query_loss, query_gradient_rows

    query_loss, query_gradient_rows = lax.map(per_block, (query_blocks, candidate_block_table, slots_all, rows_all))
    return query_loss.reshape(NQ), query_gradient_rows.reshape(NQ, D)
```

```python
import functools

import jax
import jax.numpy as jnp
from jax import lax
from jax.experimental import pallas as pl
from jax.experimental.pallas import tpu as pltpu
from jax.sharding import PartitionSpec as P

D = 768
QB = 128
PB = 128
PBD = 8
NC = 32
QBD = 8
PAIRS = QBD * NC
DEPTH = 8
SCALE = D ** (-0.5)
LOW = -1e30


def unpack(code):
    return code // 2048, (code // 32) % 64, code % 32


def fetch_loop(codes, count, blocks, buf, sems, body):
    n = count[0]

    def copy(i):
        _, owner, _ = unpack(codes[i])
        slot = lax.rem(i, DEPTH)
        return pltpu.make_async_copy(blocks.at[owner], buf.at[slot], sems.at[slot])

    def start(i, _):
        copy(i).start()
        return 0

    lax.fori_loop(0, jnp.minimum(n, DEPTH), start, 0)

    def step(i, _):
        copy(i).wait()
        body(i, buf.at[lax.rem(i, DEPTH)])

        @pl.when(i + DEPTH < n)
        def _():
            copy(i + DEPTH).start()

        return 0

    lax.fori_loop(0, n, step, 0)


def stats_kernel(codes, count, queries, pos_slot, pos_row, blocks, top, total, positive, buf, sems):
    top[...] = jnp.full_like(top, LOW)
    total[...] = jnp.zeros_like(total)
    positive[...] = jnp.zeros_like(positive)

    def body(i, block):
        e, _, slot = unpack(codes[i])
        q = queries[pl.ds(pl.multiple_of(e * QB, QB), QB), :]
        s = lax.dot_general(
            block[...], q, (((1,), (1,)), ((), ())), preferred_element_type=jnp.float32
        ) * SCALE
        row = pl.ds(e, 1)
        old = top[row, :]
        new = jnp.maximum(old, jnp.max(s, axis=0, keepdims=True))
        top[row, :] = new
        total[row, :] = total[row, :] * jnp.exp(old - new) + jnp.sum(
            jnp.exp(s - new), axis=0, keepdims=True
        )
        hit = (lax.broadcasted_iota(jnp.int32, (PB, QB), 0) == pos_row[row, :]) & (
            pos_slot[row, :] == slot
        )
        positive[row, :] += jnp.sum(jnp.where(hit, s, 0.0), axis=0, keepdims=True)

    fetch_loop(codes, count, blocks, buf, sems, body)


def sums_kernel(
    codes, count, queries, pos_slot, pos_row, row_top, row_total, blocks, out, buf, sems
):
    out[...] = jnp.zeros_like(out)

    def body(i, block):
        e, _, slot = unpack(codes[i])
        rows = pl.ds(pl.multiple_of(e * QB, QB), QB)
        q = queries[rows, :]
        b = block[...]
        s = lax.dot_general(
            q, b, (((1,), (1,)), ((), ())), preferred_element_type=jnp.float32
        ) * SCALE
        w = (jnp.exp(s - row_top[rows, :]) / row_total[rows, :]).astype(jnp.bfloat16)
        hit = (lax.broadcasted_iota(jnp.int32, (QB, PB), 1) == pos_row[rows, :]) & (
            pos_slot[rows, :] == slot
        )
        pick = jnp.where(hit, 1.0, 0.0).astype(jnp.bfloat16)
        both = jnp.dot(
            jnp.concatenate([w, pick], axis=0), b, preferred_element_type=jnp.float32
        )
        out[rows, :] += both[:QB] - both[QB:]

    fetch_loop(codes, count, blocks, buf, sems, body)


VMEM = pl.BlockSpec(memory_space=pltpu.VMEM)
SMEM = pl.BlockSpec(memory_space=pltpu.SMEM)
HBM = pl.BlockSpec(memory_space=pl.ANY)
SCRATCH = [pltpu.VMEM((DEPTH, PB, D), jnp.bfloat16), pltpu.SemaphoreType.DMA((DEPTH,))]
PARAMS = pltpu.CompilerParams(vmem_limit_bytes=24 * 1024 * 1024)


def on_device(queries, pool, candidate_block_table, pos_slot, pos_row):
    c = lax.axis_index("cand")
    mine = lax.dynamic_slice_in_dim(pool, c * PB, PB, 0)
    blocks = lax.all_gather(mine, "corpus", axis=0, tiled=False)

    table = lax.all_gather(candidate_block_table, "cand", axis=1, tiled=True)
    flat = table.reshape(PAIRS)
    number = jnp.arange(PAIRS, dtype=jnp.int32)
    held = flat % PBD == c
    rank = jnp.sum((held[None, :] & (number[None, :] < number[:, None])).astype(jnp.int32), axis=1)
    code = (number // NC) * 2048 + (flat // PBD) * 32 + number % NC
    place = held[None, :] & (rank[None, :] == number[:, None])
    codes = jnp.sum(jnp.where(place, code[None, :], 0), axis=1)
    count = jnp.sum(held.astype(jnp.int32), keepdims=True)

    stat = jax.ShapeDtypeStruct((QBD, QB), jnp.float32)
    top, total, positive = pl.pallas_call(
        stats_kernel,
        out_shape=(stat, stat, stat),
        in_specs=[SMEM, SMEM, VMEM, VMEM, VMEM, HBM],
        out_specs=(VMEM, VMEM, VMEM),
        scratch_shapes=SCRATCH,
        compiler_params=PARAMS,
        name="stats",
    )(codes, count, queries, pos_slot.reshape(QBD, QB), pos_row.reshape(QBD, QB), blocks)

    stats = lax.all_gather(jnp.stack([top, total, positive]), "cand", axis=0, tiled=False)
    row_top = jnp.max(stats[:, 0], axis=0)
    row_total = jnp.sum(stats[:, 1] * jnp.exp(stats[:, 0] - row_top), axis=0)
    query_loss = (row_top + jnp.log(row_total) - jnp.sum(stats[:, 2], axis=0)).reshape(QBD * QB)

    column = lambda a: a.reshape(QBD * QB, 1)
    partial = pl.pallas_call(
        sums_kernel,
        out_shape=jax.ShapeDtypeStruct((QBD * QB, D), jnp.float32),
        in_specs=[SMEM, SMEM, VMEM, VMEM, VMEM, VMEM, VMEM, HBM],
        out_specs=VMEM,
        scratch_shapes=SCRATCH,
        compiler_params=PARAMS,
        name="sums",
    )(
        codes, count, queries, column(pos_slot), column(pos_row),
        column(row_top), column(row_total), blocks,
    )
    gradient = lax.psum_scatter(partial, "cand", scatter_dimension=0, tiled=True)
    return (query_loss, gradient)


def solution(mesh):
    in_specs = (P("corpus", None), P("corpus", None), P("corpus", "cand"), P("corpus"), P("corpus"))
    out_specs = (P("corpus"), P(("corpus", "cand"), None))
    return jax.shard_map(
        on_device, mesh=mesh, in_specs=in_specs, out_specs=out_specs, check_vma=False
    )
```

```python
import jax
import jax.numpy as jnp
from jax import lax
from jax.experimental import pallas as pl
from jax.experimental.pallas import tpu as pltpu
from jax.sharding import PartitionSpec as P

D = 768
QB = 128
PB = 128
PBD = 8
NC = 32
QBD = 8
PAIRS = QBD * NC
NX = 4
NZ = 16
NY = 4
ROWS_A = 48
ROWS_B = PB - ROWS_A
GROUP = 4
SLOTS = 4
SCALE = D ** (-0.5)
LOW = -1e30


def for_pairs(codes, low, high, blocks_a, blocks_b, buf, sems, body):
    groups = (high - low + GROUP - 1) // GROUP

    def code(g, u):
        return codes[jnp.minimum(low + g * GROUP + u, high - 1)]

    def copies(g):
        slot = lax.rem(g, SLOTS)
        out = []
        for u in range(GROUP):
            place = (code(g, u) >> 5) & 63
            out.append(
                pltpu.make_async_copy(
                    blocks_a.at[place], buf.at[slot, u, pl.ds(0, ROWS_A)], sems.at[slot, u, 0]
                )
            )
            out.append(
                pltpu.make_async_copy(
                    blocks_b.at[place], buf.at[slot, u, pl.ds(ROWS_A, ROWS_B)], sems.at[slot, u, 1]
                )
            )
        return out

    def start(g, _):
        for c in copies(g):
            c.start()
        return 0

    lax.fori_loop(0, jnp.minimum(groups, SLOTS), start, 0)

    def step(g, _):
        for c in copies(g):
            c.wait()
        slot = lax.rem(g, SLOTS)
        body(slot, [code(g, u) for u in range(GROUP)], [low + g * GROUP + u < high for u in range(GROUP)])

        @pl.when(g + SLOTS < groups)
        def _():
            start(g + SLOTS, 0)

        return 0

    lax.fori_loop(0, groups, step, 0)


def score_of(queries, block, e):
    q = queries[pl.ds(pl.multiple_of(e * QB, QB), QB), :]
    return lax.dot_general(
        block, q, (((1,), (1,)), ((), ())), preferred_element_type=jnp.float32
    ) * SCALE


def positive_of(pos_slot, pos_row, e, slot):
    row = pl.ds(e, 1)
    return (lax.broadcasted_iota(jnp.int32, (PB, QB), 0) == pos_row[row, :]) & (
        pos_slot[row, :] == slot
    )


def stats_kernel(
    codes, ends, queries, pos_slot, pos_row, blocks_a, blocks_b, out, tops, totals, hits, buf, sems
):
    tops[...] = jnp.full_like(tops, LOW)
    totals[...] = jnp.zeros_like(totals)
    hits[...] = jnp.zeros_like(hits)

    def body(place, code, valid):
        for u in range(GROUP):
            e, slot = code[u] >> 11, code[u] & 31
            s = score_of(queries, buf[place, u], e)
            top = jnp.max(s, axis=0, keepdims=True)
            row = pl.ds(jnp.where(valid[u], code[u] >> 11 << 5 | slot, PAIRS), 1)
            tops[row, :] = top
            totals[row, :] = jnp.sum(jnp.exp(s - top), axis=0, keepdims=True)
            hit = positive_of(pos_slot, pos_row, e, slot)
            hits[row, :] = jnp.sum(jnp.where(hit, s, 0.0), axis=0, keepdims=True)

    for_pairs(codes, 0, ends[1], blocks_a, blocks_b, buf, sems, body)
    for e in range(QBD):
        rows = pl.ds(e * NC, NC)
        top = jnp.max(tops[rows, :], axis=0, keepdims=True)
        out[0, pl.ds(e, 1), :] = top
        out[1, pl.ds(e, 1), :] = jnp.sum(
            totals[rows, :] * jnp.exp(tops[rows, :] - top), axis=0, keepdims=True
        )
        out[2, pl.ds(e, 1), :] = jnp.sum(hits[rows, :], axis=0, keepdims=True)


def sums_kernel(half):
    def kernel(
        codes, ends, queries, pos_slot, pos_row, row_top, row_scale, blocks_a, blocks_b, out, buf, sems
    ):
        out[...] = jnp.zeros_like(out)

        def body(place, code, valid):
            for u in range(GROUP):
                e, slot = code[u] >> 11, code[u] & 31
                block = buf[place, u]
                s = score_of(queries, block, e)
                row = pl.ds(e, 1)
                keep = jnp.where(valid[u], 1.0, 0.0)
                w = jnp.exp(s - row_top[row, :]) * (row_scale[row, :] * keep)
                hit = positive_of(pos_slot, pos_row, e, jnp.where(valid[u], slot, -1))
                both = jnp.concatenate([w, jnp.where(hit, 1.0, 0.0)], axis=1).astype(jnp.bfloat16)
                terms = lax.dot_general(
                    both, block, (((0,), (0,)), ((), ())), preferred_element_type=jnp.float32
                )
                rows = pl.ds(pl.multiple_of((e >> 1) * QB, QB), QB)
                out[rows, :] += terms[:QB] - terms[QB:]

        for_pairs(codes, ends[half - 1] if half else 0, ends[half], blocks_a, blocks_b, buf, sems, body)

    return kernel


VMEM = pl.BlockSpec(memory_space=pltpu.VMEM)
SMEM = pl.BlockSpec(memory_space=pltpu.SMEM)
HBM = pl.BlockSpec(memory_space=pl.ANY)
FETCH = [
    pltpu.VMEM((SLOTS, GROUP, PB, D), jnp.bfloat16),
    pltpu.SemaphoreType.DMA((SLOTS, GROUP, 2)),
]
PARAMS = pltpu.CompilerParams(vmem_limit_bytes=56 * 1024 * 1024)


def shift_x(a, by):
    return lax.ppermute(
        a, "corpus", [(x * NZ + z, (x + by) % NX * NZ + z) for x in range(NX) for z in range(NZ)]
    )


def shift_z(a, by):
    return lax.ppermute(
        a, "corpus", [(x * NZ + z, x * NZ + (z + by) % NZ) for x in range(NX) for z in range(NZ)]
    )


def gather_pool(mine):
    a, b = mine[:ROWS_A], mine[ROWS_A:]
    a4 = jnp.stack([a, shift_x(a, 1), shift_x(a, 2), shift_x(a, -1)])
    parts_a, parts_b = {0: a4}, {0: b}
    for k in range(1, NZ // 2 + 1):
        parts_b[k] = shift_z(parts_b[k - 1], 1)
        if k < NZ // 2:
            parts_b[-k] = shift_z(parts_b[1 - k], -1)
    for k in range(1, NZ // 2 + 1):
        parts_a[k] = shift_z(parts_a[k - 1], 1)
        if k < NZ // 2:
            parts_a[-k] = shift_z(parts_a[1 - k], -1)
    blocks_a = jnp.zeros((NZ, NX, ROWS_A, D), jnp.bfloat16)
    for k in parts_a:
        blocks_a = lax.dynamic_update_slice(blocks_a, parts_a[k][None], (k + 7, 0, 0, 0))
    blocks_b = jnp.zeros((NZ, NX, ROWS_B, D), jnp.bfloat16)

    def put(blocks, piece, ks, j):
        for n, k in enumerate(ks):
            blocks = lax.dynamic_update_slice(blocks, piece[n][None, None], (k + 7, j, 0, 0))
        return blocks

    for right, left in (((0, 1, 2), (-2, -1)), ((3, 4, 5), (-5, -4, -3)), ((6, 7, 8), (-7, -6))):
        pr, pb = jnp.stack([parts_b[k] for k in right]), jnp.stack([parts_b[k] for k in left])
        blocks_b = put(blocks_b, pr, right, 0)
        blocks_b = put(blocks_b, pb, left, 0)
        r1, b1 = shift_x(pr, 1), shift_x(pb, 1)
        r3, b3 = shift_x(pr, -1), shift_x(pb, -1)
        r2, b2 = shift_x(r1, 1), shift_x(b3, -1)
        for j, r, l in ((1, r1, b1), (3, r3, b3), (2, r2, b2)):
            blocks_b = put(blocks_b, r, right, j)
            blocks_b = put(blocks_b, l, left, j)
    return (
        blocks_a.reshape(NZ * NX, ROWS_A, D),
        blocks_b.reshape(NZ * NX, ROWS_B, D),
    )


def on_device(queries, pool, candidate_block_table, pos_slot, pos_row):
    c = lax.axis_index("cand")
    core = c % 2
    corpus = lax.axis_index("corpus")
    mine = lax.dynamic_slice_in_dim(pool, c * PB, PB, 0)
    blocks_a, blocks_b = gather_pool(mine)

    table = lax.all_gather(candidate_block_table, "cand", axis=1, tiled=True)
    flat = table.reshape(PAIRS)
    number = jnp.arange(PAIRS, dtype=jnp.int32)
    e = number // NC
    held = flat % PBD == c
    first = e % 2 != core
    order = number + jnp.where(first, 0, PAIRS)
    rank = jnp.sum((held[None, :] & (order[None, :] < order[:, None])).astype(jnp.int32), axis=1)
    owner = flat // PBD
    p = (corpus % NZ - owner % NZ + 7) % NZ
    j = (corpus // NZ - owner // NZ) % NX
    code = e * 2048 + (p * NX + j) * 32 + number % NC
    place = held[None, :] & (rank[None, :] == number[:, None])
    codes = jnp.sum(jnp.where(place, code[None, :], 0), axis=1)
    ends = jnp.stack(
        [jnp.sum((held & first).astype(jnp.int32)), jnp.sum(held.astype(jnp.int32))]
    )

    slots, rows = pos_slot.reshape(QBD, QB), pos_row.reshape(QBD, QB)
    mine_stats = pl.pallas_call(
        stats_kernel,
        out_shape=jax.ShapeDtypeStruct((3, QBD, QB), jnp.float32),
        in_specs=[SMEM, SMEM, VMEM, VMEM, VMEM, HBM, HBM],
        out_specs=VMEM,
        scratch_shapes=[pltpu.VMEM((PAIRS + 8, QB), jnp.float32)] * 3 + FETCH,
        compiler_params=PARAMS,
        name="stats",
    )(codes, ends, queries, slots, rows, blocks_a, blocks_b)

    stats = lax.all_gather(mine_stats, "cand", axis=0, tiled=False)
    row_top = jnp.max(stats[:, 0], axis=0)
    row_total = jnp.sum(stats[:, 1] * jnp.exp(stats[:, 0] - row_top), axis=0)
    query_loss = (row_top + jnp.log(row_total) - jnp.sum(stats[:, 2], axis=0)).reshape(QBD * QB)

    def sums(half):
        return pl.pallas_call(
            sums_kernel(half),
            out_shape=jax.ShapeDtypeStruct((QBD * QB // 2, D), jnp.float32),
            in_specs=[SMEM, SMEM, VMEM, VMEM, VMEM, VMEM, VMEM, HBM, HBM],
            out_specs=VMEM,
            scratch_shapes=FETCH,
            compiler_params=PARAMS,
            cost_estimate=pl.CostEstimate(flops=10**9, bytes_accessed=10**7, transcendentals=0),
            name="sums",
        )(codes, ends, queries, slots, rows, row_top, 1.0 / row_total, blocks_a, blocks_b)

    sent = lax.ppermute(sums(0), "cand", [(i, i ^ 1) for i in range(2 * NY)])
    both = (sums(1) + sent).reshape(NY, QB, D)
    groups = [[2 * y + k for y in range(NY)] for k in range(2)]
    parts = lax.all_to_all(both, "cand", split_axis=0, concat_axis=0, axis_index_groups=groups, tiled=True)
    return (query_loss, jnp.sum(parts, axis=0))


def solution(mesh):
    in_specs = (P("corpus", None), P("corpus", None), P("corpus", "cand"), P("corpus"), P("corpus"))
    out_specs = (P("corpus"), P(("corpus", "cand"), None))
    return jax.shard_map(
        on_device, mesh=mesh, in_specs=in_specs, out_specs=out_specs, check_vma=False
    )
```

```python
import jax
import jax.numpy as jnp
from jax import lax
from jax.experimental import pallas as pl
from jax.experimental.pallas import tpu as pltpu
from jax.sharding import PartitionSpec as P

D = 768
QB = 128
PB = 128
PBD = 8
NC = 32
QBD = 8
PAIRS = QBD * NC
NX = 4
NZ = 16
NY = 4
ROWS_A = 64
ROWS_B = PB - ROWS_A
GROUP = 4
SLOTS = 4
SCALE = D ** (-0.5)
LOW = -1e30


def for_groups(codes, low, high, blocks_a, blocks_b, buf, sems, body):
    def copies(g):
        slot = lax.rem(g, SLOTS)
        out = []
        for u in range(GROUP):
            code = codes[g * GROUP + u]
            owner, place = (code >> 6) & 63, (code >> 12) & 63
            out.append(
                pltpu.make_async_copy(
                    blocks_a.at[owner], buf.at[slot, pl.ds(u * PB, ROWS_A)], sems.at[slot, u, 0]
                )
            )
            out.append(
                pltpu.make_async_copy(
                    blocks_b.at[place],
                    buf.at[slot, pl.ds(u * PB + ROWS_A, ROWS_B)],
                    sems.at[slot, u, 1],
                )
            )
        return out

    def start(g, _):
        for c in copies(g):
            c.start()
        return 0

    lax.fori_loop(low, jnp.minimum(high, low + SLOTS), start, 0)

    def step(g, _):
        for c in copies(g):
            c.wait()
        code = [codes[g * GROUP + u] for u in range(GROUP)]
        body(lax.rem(g, SLOTS), code[0] >> 18, [(c & 63) - 1 for c in code])

        @pl.when(g + SLOTS < high)
        def _():
            start(g + SLOTS, 0)

        return 0

    lax.fori_loop(low, high, step, 0)


def scores_of(queries, block, e):
    q = queries[pl.ds(pl.multiple_of(e * QB, QB), QB), :]
    return lax.dot_general(
        block, q, (((1,), (1,)), ((), ())), preferred_element_type=jnp.float32
    ) * SCALE


def per_slot(slots, f):
    return jnp.concatenate([f(s) for s in slots], axis=0)


def positive_of(pos_slot, pos_row, e, slots):
    row = pl.ds(e, 1)
    here = lax.broadcasted_iota(jnp.int32, (PB, QB), 0) == pos_row[row, :]
    return per_slot(slots, lambda s: jnp.where(here & (pos_slot[row, :] == s), 1.0, 0.0))


def stats_kernel(
    codes, ends, queries, pos_slot, pos_row, blocks_a, blocks_b, out, buf, sems
):
    out[0] = jnp.full((QBD, QB), LOW, jnp.float32)
    out[1] = jnp.zeros((QBD, QB), jnp.float32)
    out[2] = jnp.zeros((QBD, QB), jnp.float32)

    def body(place, e, slots):
        s = scores_of(queries, buf[place], e)
        valid = per_slot(slots, lambda t: jnp.full((PB, QB), t, jnp.int32)) >= 0
        row = pl.ds(e, 1)
        old = out[0, row, :]
        top = jnp.maximum(old, jnp.max(jnp.where(valid, s, LOW), axis=0, keepdims=True))
        terms = jnp.where(valid, jnp.exp(jnp.minimum(s - top, 0.0)), 0.0)
        hit = positive_of(pos_slot, pos_row, e, slots)
        out[0, row, :] = top
        out[1, row, :] = out[1, row, :] * jnp.exp(old - top) + jnp.sum(terms, axis=0, keepdims=True)
        out[2, row, :] += jnp.sum(hit * s, axis=0, keepdims=True)

    for_groups(codes, 0, ends[1], blocks_a, blocks_b, buf, sems, body)


def sums_kernel(half):
    def kernel(
        codes, ends, queries, pos_slot, pos_row, row_top, row_scale, blocks_a, blocks_b, out, buf, sems
    ):
        out[...] = jnp.zeros_like(out)

        def body(place, e, slots):
            block = buf[place]
            s = scores_of(queries, block, e)
            row = pl.ds(e, 1)
            valid = per_slot(slots, lambda t: jnp.full((PB, QB), t, jnp.int32)) >= 0
            w = jnp.exp(jnp.minimum(s - row_top[row, :], 0.0)) * row_scale[row, :]
            w = jnp.where(valid, w, 0.0)
            hit = positive_of(pos_slot, pos_row, e, slots)
            terms = lax.dot_general(
                jnp.concatenate([w.astype(jnp.bfloat16), (-hit).astype(jnp.bfloat16)], axis=0),
                jnp.concatenate([block, block], axis=0),
                (((0,), (0,)), ((), ())),
                preferred_element_type=jnp.float32,
            )
            rows = pl.ds(pl.multiple_of((e >> 1) * QB, QB), QB)
            out[rows, :] += terms

        for_groups(codes, ends[0] if half else 0, ends[half], blocks_a, blocks_b, buf, sems, body)

    return kernel


VMEM = pl.BlockSpec(memory_space=pltpu.VMEM)
SMEM = pl.BlockSpec(memory_space=pltpu.SMEM)
HBM = pl.BlockSpec(memory_space=pl.ANY)
FETCH = [
    pltpu.VMEM((SLOTS, GROUP * PB, D), jnp.bfloat16),
    pltpu.SemaphoreType.DMA((SLOTS, GROUP, 2)),
]
PARAMS = pltpu.CompilerParams(vmem_limit_bytes=56 * 1024 * 1024)


def shift_x(a, by):
    return lax.ppermute(
        a, "corpus", [(x * NZ + z, (x + by) % NX * NZ + z) for x in range(NX) for z in range(NZ)]
    )


def shift_z(a, by):
    return lax.ppermute(
        a, "corpus", [(x * NZ + z, x * NZ + (z + by) % NZ) for x in range(NX) for z in range(NZ)]
    )


def gather_pool(mine):
    blocks_a = lax.all_gather(mine[:ROWS_A], "corpus", axis=0, tiled=False)
    b = mine[ROWS_A:]
    parts = {0: jnp.stack([b, shift_x(b, 1), shift_x(b, 2), shift_x(b, -1)])}
    for k in range(1, NZ // 2 + 1):
        parts[k] = shift_z(parts[k - 1], 1)
        if k < NZ // 2:
            parts[-k] = shift_z(parts[1 - k], -1)
    blocks_b = jnp.zeros((NZ, NX, ROWS_B, D), jnp.bfloat16)
    for k in parts:
        blocks_b = lax.dynamic_update_slice(blocks_b, parts[k][None], (k + 7, 0, 0, 0))
    return blocks_a, blocks_b.reshape(NZ * NX, ROWS_B, D)


def on_device(queries, pool, candidate_block_table, pos_slot, pos_row):
    c = lax.axis_index("cand")
    core = c % 2
    corpus = lax.axis_index("corpus")
    mine = lax.dynamic_slice_in_dim(pool, c * PB, PB, 0)
    blocks_a, blocks_b = gather_pool(mine)

    table = lax.all_gather(candidate_block_table, "cand", axis=1, tiled=True)
    flat = table.reshape(PAIRS)
    number = jnp.arange(PAIRS, dtype=jnp.int32)
    held = flat % PBD == c
    owner = flat // PBD
    p = (corpus % NZ - owner % NZ + 7) % NZ
    j = (corpus // NZ - owner // NZ) % NX
    e = number // NC
    code = e * 2**18 + (p * NX + j) * 2**12 + owner * 2**6 + number % NC + 1
    by_e = held.reshape(QBD, NC).astype(jnp.int32)
    padded = (jnp.sum(by_e, axis=1) + GROUP - 1) // GROUP * GROUP
    block = jnp.arange(QBD)
    later = (block % 2 == core).astype(jnp.int32)
    turn = block + QBD * later
    base = jnp.sum(jnp.where(turn[None, :] < turn[:, None], padded[None, :], 0), axis=1)
    before = number[:NC, None] > number[None, :NC]
    rank = jnp.sum(jnp.where(before[None], by_e[:, None, :], 0), axis=2)
    position = (base[:, None] + rank).reshape(PAIRS)
    place = held[None, :] & (position[None, :] == number[:, None])
    codes = jnp.sum(jnp.where(place, code[None, :], 0), axis=1)
    ends = jnp.stack([jnp.sum(padded * (1 - later)), jnp.sum(padded)]) // GROUP

    slots, rows = pos_slot.reshape(QBD, QB), pos_row.reshape(QBD, QB)
    mine_stats = pl.pallas_call(
        stats_kernel,
        out_shape=jax.ShapeDtypeStruct((3, QBD, QB), jnp.float32),
        in_specs=[SMEM, SMEM, VMEM, VMEM, VMEM, HBM, HBM],
        out_specs=VMEM,
        scratch_shapes=FETCH,
        compiler_params=PARAMS,
        name="stats",
    )(codes, ends, queries, slots, rows, blocks_a, blocks_b)

    stats = lax.all_gather(mine_stats, "cand", axis=0, tiled=False)
    row_top = jnp.max(stats[:, 0], axis=0)
    row_total = jnp.sum(stats[:, 1] * jnp.exp(stats[:, 0] - row_top), axis=0)
    query_loss = (row_top + jnp.log(row_total) - jnp.sum(stats[:, 2], axis=0)).reshape(QBD * QB)

    def sums(half):
        return pl.pallas_call(
            sums_kernel(half),
            out_shape=jax.ShapeDtypeStruct((QBD * QB // 2, D), jnp.float32),
            in_specs=[SMEM, SMEM, VMEM, VMEM, VMEM, VMEM, VMEM, HBM, HBM],
            out_specs=VMEM,
            scratch_shapes=FETCH,
            compiler_params=PARAMS,
            cost_estimate=pl.CostEstimate(flops=10**9, bytes_accessed=10**7, transcendentals=0),
            name="sums",
        )(codes, ends, queries, slots, rows, row_top, 1.0 / row_total, blocks_a, blocks_b)

    sent = lax.ppermute(sums(0), "cand", [(i, i ^ 1) for i in range(2 * NY)])
    both = (sums(1) + sent).reshape(NY, QB, D)
    groups = [[2 * y + k for y in range(NY)] for k in range(2)]
    parts = lax.all_to_all(both, "cand", split_axis=0, concat_axis=0, axis_index_groups=groups, tiled=True)
    return (query_loss, jnp.sum(parts, axis=0))


def solution(mesh):
    in_specs = (P("corpus", None), P("corpus", None), P("corpus", "cand"), P("corpus"), P("corpus"))
    out_specs = (P("corpus"), P(("corpus", "cand"), None))
    return jax.shard_map(
        on_device, mesh=mesh, in_specs=in_specs, out_specs=out_specs, check_vma=False
    )
```

```python
import jax
import jax.numpy as jnp
from jax import lax
from jax.experimental import pallas as pl
from jax.experimental.pallas import tpu as pltpu
from jax.sharding import PartitionSpec as P

D = 768
QB = 128
PB = 128
PBD = 8
NC = 32
QBD = 8
PAIRS = QBD * NC
NX = 4
NZ = 16
NY = 4
ROWS_A = 64
ROWS_B = PB - ROWS_A
GROUP = 2
SLOTS = 6
SCALE = D ** (-0.5)
LOW = -1e30


def for_groups(codes, low, high, blocks_a, blocks_b, buf, sems, body):
    def start(g, _):
        slot = lax.rem(g, SLOTS)
        for u in range(GROUP):
            code = codes[g * GROUP + u]
            a, b = (code >> 6) & 63, (code >> 12) & 63
            pltpu.make_async_copy(
                blocks_a.at[a], buf.at[slot, pl.ds(u * PB, ROWS_A)], sems.at[slot]
            ).start()
            pltpu.make_async_copy(
                blocks_b.at[b], buf.at[slot, pl.ds(u * PB + ROWS_A, ROWS_B)], sems.at[slot]
            ).start()
        return 0

    lax.fori_loop(low, jnp.minimum(high, low + SLOTS), start, 0)

    def step(g, _):
        slot = lax.rem(g, SLOTS)
        pltpu.make_async_copy(buf.at[slot], buf.at[slot], sems.at[slot]).wait()
        code = [codes[g * GROUP + u] for u in range(GROUP)]
        body(slot, code[0] >> 18, [(c & 63) - 1 for c in code])

        @pl.when(g + SLOTS < high)
        def _():
            start(g + SLOTS, 0)

        return 0

    lax.fori_loop(low, high, step, 0)


def scores_of(queries, block, e):
    q = queries[pl.ds(pl.multiple_of(e * QB, QB), QB), :]
    return lax.dot_general(
        block, q, (((1,), (1,)), ((), ())), preferred_element_type=jnp.float32
    ) * SCALE


def per_slot(slots, f):
    return jnp.concatenate([f(s) for s in slots], axis=0)


def positive_of(pos_slot, pos_row, e, slots):
    row = pl.ds(e, 1)
    here = lax.broadcasted_iota(jnp.int32, (PB, QB), 0) == pos_row[row, :]
    return per_slot(slots, lambda s: jnp.where(here & (pos_slot[row, :] == s), 1.0, 0.0))


def stats_kernel(
    codes, ends, queries, pos_slot, pos_row, blocks_a, blocks_b, out, buf, sems
):
    out[0] = jnp.full((QBD, QB), LOW, jnp.float32)
    out[1] = jnp.zeros((QBD, QB), jnp.float32)
    out[2] = jnp.zeros((QBD, QB), jnp.float32)

    def body(place, e, slots):
        s = scores_of(queries, buf[place], e)
        valid = per_slot(slots, lambda t: jnp.full((PB, QB), t, jnp.int32)) >= 0
        row = pl.ds(e, 1)
        old = out[0, row, :]
        top = jnp.maximum(old, jnp.max(jnp.where(valid, s, LOW), axis=0, keepdims=True))
        terms = jnp.where(valid, jnp.exp(jnp.minimum(s - top, 0.0)), 0.0)
        hit = positive_of(pos_slot, pos_row, e, slots)
        out[0, row, :] = top
        out[1, row, :] = out[1, row, :] * jnp.exp(old - top) + jnp.sum(terms, axis=0, keepdims=True)
        out[2, row, :] += jnp.sum(hit * s, axis=0, keepdims=True)

    for_groups(codes, 0, ends[1], blocks_a, blocks_b, buf, sems, body)


def sums_kernel(half):
    def kernel(
        codes, ends, queries, pos_slot, pos_row, row_top, row_scale, blocks_a, blocks_b, out, buf, sems
    ):
        out[...] = jnp.zeros_like(out)

        def body(place, e, slots):
            block = buf[place]
            s = scores_of(queries, block, e)
            row = pl.ds(e, 1)
            valid = per_slot(slots, lambda t: jnp.full((PB, QB), t, jnp.int32)) >= 0
            w = jnp.exp(jnp.minimum(s - row_top[row, :], 0.0)) * row_scale[row, :]
            w = jnp.where(valid, w, 0.0)
            hit = positive_of(pos_slot, pos_row, e, slots)
            terms = lax.dot_general(
                jnp.concatenate([w, hit], axis=1).astype(jnp.bfloat16),
                block,
                (((0,), (0,)), ((), ())),
                preferred_element_type=jnp.float32,
            )
            rows = pl.ds(pl.multiple_of((e >> 1) * QB, QB), QB)
            out[rows, :] += terms[:QB] - terms[QB:]

        for_groups(codes, ends[0] if half else 0, ends[half], blocks_a, blocks_b, buf, sems, body)

    return kernel


VMEM = pl.BlockSpec(memory_space=pltpu.VMEM)
SMEM = pl.BlockSpec(memory_space=pltpu.SMEM)
HBM = pl.BlockSpec(memory_space=pl.ANY)
FETCH = [
    pltpu.VMEM((SLOTS, GROUP * PB, D), jnp.bfloat16),
    pltpu.SemaphoreType.DMA((SLOTS,)),
]
PARAMS = pltpu.CompilerParams(vmem_limit_bytes=56 * 1024 * 1024)


def shift(a, dx, dz):
    pairs = []
    for x in range(NX):
        for z in range(NZ):
            for c in range(2 * NY):
                sign = 1 - 2 * (c % 2)
                to = (x + sign * dx) % NX * NZ + (z + sign * dz) % NZ
                pairs.append(((x * NZ + z) * 2 * NY + c, to * 2 * NY + c))
    return lax.ppermute(a, ("corpus", "cand"), pairs)


X_GROUPS = [[x * NZ + z for x in range(NX)] for z in range(NZ)]
BATCHES = ((0, 5), (5, 10), (10, 16))


def gather_pool(mine):
    a, b = mine[:ROWS_A], mine[ROWS_A:]
    single = [b]
    for k in range(1, NZ):
        single.append(shift(single[-1], 0, 1))
    four = jnp.stack([a] + [shift(a, j, 0) for j in range(1, NX)])
    blocks_b = jnp.zeros((NX, NZ, ROWS_B, D), jnp.bfloat16)
    for low, high in BATCHES:
        piece = lax.all_gather(
            jnp.stack(single[low:high]), "corpus", axis=0, axis_index_groups=X_GROUPS, tiled=False
        )
        blocks_b = lax.dynamic_update_slice(blocks_b, piece, (0, low, 0, 0))
    middle = four
    blocks_a = jnp.zeros((NZ, NX, ROWS_A, D), jnp.bfloat16)
    blocks_a = lax.dynamic_update_slice(blocks_a, four[None], (0, 0, 0, 0))
    for k in range(1, NZ):
        four, _ = lax.optimization_barrier((four, single[min(2 * k, NZ - 1)]))
        four = shift(four, 0, 1)
        middle = four if k == 10 else middle
        blocks_a = lax.dynamic_update_slice(blocks_a, four[None], (k, 0, 0, 0))
    return blocks_a.reshape(NZ * NX, ROWS_A, D), blocks_b.reshape(NX * NZ, ROWS_B, D), middle


def on_device(queries, pool, candidate_block_table, pos_slot, pos_row):
    c = lax.axis_index("cand")
    core = c % 2
    corpus = lax.axis_index("corpus")
    mine = lax.dynamic_slice_in_dim(pool, c * PB, PB, 0)
    blocks_a, blocks_b, middle = gather_pool(mine)
    candidate_block_table, _ = lax.optimization_barrier((candidate_block_table, middle))

    table = lax.all_gather(candidate_block_table, "cand", axis=1, tiled=True)
    flat = table.reshape(PAIRS)
    number = jnp.arange(PAIRS, dtype=jnp.int32)
    held = flat % PBD == c
    owner = flat // PBD
    sign = 1 - 2 * core
    k = (sign * (corpus % NZ - owner % NZ)) % NZ
    j = (sign * (corpus // NZ - owner // NZ)) % NX
    e = number // NC
    code = e * 2**18 + (owner // NZ * NZ + k) * 2**12 + (k * NX + j) * 2**6 + number % NC + 1
    by_e = held.reshape(QBD, NC).astype(jnp.int32)
    padded = (jnp.sum(by_e, axis=1) + GROUP - 1) // GROUP * GROUP
    block = jnp.arange(QBD)
    later = (block % 2 == core).astype(jnp.int32)
    turn = block + QBD * later
    base = jnp.sum(jnp.where(turn[None, :] < turn[:, None], padded[None, :], 0), axis=1)
    before = number[:NC, None] > number[None, :NC]
    rank = jnp.sum(jnp.where(before[None], by_e[:, None, :], 0), axis=2)
    position = (base[:, None] + rank).reshape(PAIRS)
    place = held[None, :] & (position[None, :] == number[:, None])
    codes = jnp.sum(jnp.where(place, code[None, :], 0), axis=1)
    ends = jnp.stack([jnp.sum(padded * (1 - later)), jnp.sum(padded)]) // GROUP

    slots, rows = pos_slot.reshape(QBD, QB), pos_row.reshape(QBD, QB)
    mine_stats = pl.pallas_call(
        stats_kernel,
        out_shape=jax.ShapeDtypeStruct((3, QBD, QB), jnp.float32),
        in_specs=[SMEM, SMEM, VMEM, VMEM, VMEM, HBM, HBM],
        out_specs=VMEM,
        scratch_shapes=FETCH,
        compiler_params=PARAMS,
        name="stats",
    )(codes, ends, queries, slots, rows, blocks_a, blocks_b)

    stats = lax.all_gather(mine_stats, "cand", axis=0, tiled=False)
    row_top = jnp.max(stats[:, 0], axis=0)
    row_total = jnp.sum(stats[:, 1] * jnp.exp(stats[:, 0] - row_top), axis=0)
    query_loss = (row_top + jnp.log(row_total) - jnp.sum(stats[:, 2], axis=0)).reshape(QBD * QB)

    def sums(half):
        return pl.pallas_call(
            sums_kernel(half),
            out_shape=jax.ShapeDtypeStruct((QBD * QB // 2, D), jnp.float32),
            in_specs=[SMEM, SMEM, VMEM, VMEM, VMEM, VMEM, VMEM, HBM, HBM],
            out_specs=VMEM,
            scratch_shapes=FETCH,
            compiler_params=PARAMS,
            cost_estimate=pl.CostEstimate(flops=10**9, bytes_accessed=10**7, transcendentals=0),
            name="sums",
        )(codes, ends, queries, slots, rows, row_top, 1.0 / row_total, blocks_a, blocks_b)

    sent = lax.ppermute(sums(0), "cand", [(i, i ^ 1) for i in range(2 * NY)])
    both = (sums(1) + sent).reshape(NY, QB, D)
    groups = [[2 * y + k for y in range(NY)] for k in range(2)]
    parts = lax.all_to_all(both, "cand", split_axis=0, concat_axis=0, axis_index_groups=groups, tiled=True)
    return (query_loss, jnp.sum(parts, axis=0))


def solution(mesh):
    in_specs = (P("corpus", None), P("corpus", None), P("corpus", "cand"), P("corpus"), P("corpus"))
    out_specs = (P("corpus"), P(("corpus", "cand"), None))
    return jax.shard_map(
        on_device, mesh=mesh, in_specs=in_specs, out_specs=out_specs, check_vma=False
    )
```

```python
import jax
import jax.numpy as jnp
from jax import lax
from jax.experimental import pallas as pl
from jax.experimental.pallas import tpu as pltpu
from jax.sharding import PartitionSpec as P

D = 768
QB = 128
PB = 128
PBD = 8
NC = 32
QBD = 8
PAIRS = QBD * NC
NX = 4
NZ = 16
NY = 4
HALF = NZ // 2
ROWS_A = 48
ROWS_B = PB - ROWS_A
GROUP = 2
SLOTS = 6
SCALE = D ** (-0.5)
LOW = -1e30


def choose(refs, number, act):
    if len(refs) == 1:
        act(refs[0])
        return
    half = len(refs) // 2

    @pl.when(number < half)
    def _():
        choose(refs[:half], number, act)

    @pl.when(number >= half)
    def _():
        choose(refs[half:], number - half, act)


def for_groups(codes, low, high, blocks_a, blocks_b, buf, sems, body):
    def start(g, _):
        slot = lax.rem(g, SLOTS)
        for u in range(GROUP):
            code = codes[g * GROUP + u]
            a, part, b = (code >> 6) & 63, (code >> 15) & 7, (code >> 12) & 7
            pltpu.make_async_copy(
                blocks_a.at[a], buf.at[slot, pl.ds(u * PB, ROWS_A)], sems.at[slot]
            ).start()
            choose(
                blocks_b,
                part,
                lambda ref: pltpu.make_async_copy(
                    ref.at[b], buf.at[slot, pl.ds(u * PB + ROWS_A, ROWS_B)], sems.at[slot]
                ).start(),
            )
        return 0

    lax.fori_loop(low, jnp.minimum(high, low + SLOTS), start, 0)

    def step(g, _):
        slot = lax.rem(g, SLOTS)
        pltpu.make_async_copy(buf.at[slot], buf.at[slot], sems.at[slot]).wait()
        code = [codes[g * GROUP + u] for u in range(GROUP)]
        body(slot, code[0] >> 18, [(c & 63) - 1 for c in code])

        @pl.when(g + SLOTS < high)
        def _():
            start(g + SLOTS, 0)

        return 0

    lax.fori_loop(low, high, step, 0)


def scores_of(queries, block, e):
    q = queries[pl.ds(pl.multiple_of(e * QB, QB), QB), :]
    return lax.dot_general(
        block, q, (((1,), (1,)), ((), ())), preferred_element_type=jnp.float32
    ) * SCALE


def per_slot(slots, f):
    return jnp.concatenate([f(s) for s in slots], axis=0)


def positive_of(pos_slot, pos_row, e, slots):
    row = pl.ds(e, 1)
    here = lax.broadcasted_iota(jnp.int32, (PB, QB), 0) == pos_row[row, :]
    return per_slot(slots, lambda s: jnp.where(here & (pos_slot[row, :] == s), 1.0, 0.0))


def stats_kernel(
    codes, ends, queries, pos_slot, pos_row, blocks_a, *rest
):
    blocks_b, (out, buf, sems) = rest[:8], rest[8:]
    out[0] = jnp.full((QBD, QB), LOW, jnp.float32)
    out[1] = jnp.zeros((QBD, QB), jnp.float32)
    out[2] = jnp.zeros((QBD, QB), jnp.float32)

    def body(place, e, slots):
        s = scores_of(queries, buf[place], e)
        valid = per_slot(slots, lambda t: jnp.full((PB, QB), t, jnp.int32)) >= 0
        row = pl.ds(e, 1)
        old = out[0, row, :]
        top = jnp.maximum(old, jnp.max(jnp.where(valid, s, LOW), axis=0, keepdims=True))
        terms = jnp.where(valid, jnp.exp(jnp.minimum(s - top, 0.0)), 0.0)
        hit = positive_of(pos_slot, pos_row, e, slots)
        out[0, row, :] = top
        out[1, row, :] = out[1, row, :] * jnp.exp(old - top) + jnp.sum(terms, axis=0, keepdims=True)
        out[2, row, :] += jnp.sum(hit * s, axis=0, keepdims=True)

    for_groups(codes, 0, ends[1], blocks_a, blocks_b, buf, sems, body)


def sums_kernel(half):
    def kernel(
        codes, ends, queries, pos_slot, pos_row, row_top, row_scale, blocks_a, *rest
    ):
        blocks_b, (out, buf, sems) = rest[:8], rest[8:]
        out[...] = jnp.zeros_like(out)

        def body(place, e, slots):
            block = buf[place]
            s = scores_of(queries, block, e)
            row = pl.ds(e, 1)
            valid = per_slot(slots, lambda t: jnp.full((PB, QB), t, jnp.int32)) >= 0
            w = jnp.exp(jnp.minimum(s - row_top[row, :], 0.0)) * row_scale[row, :]
            w = jnp.where(valid, w, 0.0)
            hit = positive_of(pos_slot, pos_row, e, slots)
            terms = lax.dot_general(
                jnp.concatenate([w, hit], axis=1).astype(jnp.bfloat16),
                block,
                (((0,), (0,)), ((), ())),
                preferred_element_type=jnp.float32,
            )
            rows = pl.ds(pl.multiple_of((e >> 1) * QB, QB), QB)
            out[rows, :] += terms[:QB] - terms[QB:]

        for_groups(codes, ends[0] if half else 0, ends[half], blocks_a, blocks_b, buf, sems, body)

    return kernel


VMEM = pl.BlockSpec(memory_space=pltpu.VMEM)
SMEM = pl.BlockSpec(memory_space=pltpu.SMEM)
HBM = pl.BlockSpec(memory_space=pl.ANY)
FETCH = [
    pltpu.VMEM((SLOTS, GROUP * PB, D), jnp.bfloat16),
    pltpu.SemaphoreType.DMA((SLOTS,)),
]
PARAMS = pltpu.CompilerParams(vmem_limit_bytes=56 * 1024 * 1024)


def shift_x(a, by):
    return lax.ppermute(
        a, "corpus", [(x * NZ + z, (x + by) % NX * NZ + z) for x in range(NX) for z in range(NZ)]
    )


def gather_z(a):
    groups = [[x * NZ + z for z in range(NZ)] for x in range(NX)]
    return lax.all_gather(a, "corpus", axis=0, axis_index_groups=groups, tiled=False)


def gather_pool(mine):
    a, b = mine[:ROWS_A], mine[ROWS_A:]
    all_z = gather_z(b)
    blocks_a = gather_z(jnp.stack([a, shift_x(a, 1), shift_x(a, 2), shift_x(a, -1)]))
    low, high = all_z[:HALF], all_z[HALF:]
    right_low, left_high = shift_x(low, 1), shift_x(high, -1)
    right_high, left_low = shift_x(high, 1), shift_x(low, -1)
    far_low, far_high = shift_x(right_low, 1), shift_x(left_high, -1)
    parts = (low, high, right_low, right_high, far_low, far_high, left_low, left_high)
    return blocks_a.reshape(NZ * NX, ROWS_A, D), parts


def on_device(queries, pool, candidate_block_table, pos_slot, pos_row):
    c = lax.axis_index("cand")
    core = c % 2
    corpus = lax.axis_index("corpus")
    mine = lax.dynamic_slice_in_dim(pool, c * PB, PB, 0)
    blocks_a, blocks_b = gather_pool(mine)

    table = lax.all_gather(candidate_block_table, "cand", axis=1, tiled=True)
    flat = table.reshape(PAIRS)
    number = jnp.arange(PAIRS, dtype=jnp.int32)
    held = flat % PBD == c
    owner = flat // PBD
    j = (corpus // NZ - owner // NZ) % NX
    e = number // NC
    code = e * 2**18 + (j * NZ + owner % NZ) * 2**12 + (owner % NZ * NX + j) * 2**6 + number % NC + 1
    by_e = held.reshape(QBD, NC).astype(jnp.int32)
    padded = (jnp.sum(by_e, axis=1) + GROUP - 1) // GROUP * GROUP
    block = jnp.arange(QBD)
    later = (block % 2 == core).astype(jnp.int32)
    turn = block + QBD * later
    base = jnp.sum(jnp.where(turn[None, :] < turn[:, None], padded[None, :], 0), axis=1)
    before = number[:NC, None] > number[None, :NC]
    rank = jnp.sum(jnp.where(before[None], by_e[:, None, :], 0), axis=2)
    position = (base[:, None] + rank).reshape(PAIRS)
    place = held[None, :] & (position[None, :] == number[:, None])
    codes = jnp.sum(jnp.where(place, code[None, :], 0), axis=1)
    ends = jnp.stack([jnp.sum(padded * (1 - later)), jnp.sum(padded)]) // GROUP

    slots, rows = pos_slot.reshape(QBD, QB), pos_row.reshape(QBD, QB)
    mine_stats = pl.pallas_call(
        stats_kernel,
        out_shape=jax.ShapeDtypeStruct((3, QBD, QB), jnp.float32),
        in_specs=[SMEM, SMEM, VMEM, VMEM, VMEM] + [HBM] * 9,
        out_specs=VMEM,
        scratch_shapes=FETCH,
        compiler_params=PARAMS,
        name="stats",
    )(codes, ends, queries, slots, rows, blocks_a, *blocks_b)

    stats = lax.all_gather(mine_stats, "cand", axis=0, tiled=False)
    row_top = jnp.max(stats[:, 0], axis=0)
    row_total = jnp.sum(stats[:, 1] * jnp.exp(stats[:, 0] - row_top), axis=0)
    query_loss = (row_top + jnp.log(row_total) - jnp.sum(stats[:, 2], axis=0)).reshape(QBD * QB)

    def sums(half):
        return pl.pallas_call(
            sums_kernel(half),
            out_shape=jax.ShapeDtypeStruct((QBD * QB // 2, D), jnp.float32),
            in_specs=[SMEM, SMEM, VMEM, VMEM, VMEM, VMEM, VMEM] + [HBM] * 9,
            out_specs=VMEM,
            scratch_shapes=FETCH,
            compiler_params=PARAMS,
            cost_estimate=pl.CostEstimate(flops=10**9, bytes_accessed=10**7, transcendentals=0),
            name="sums",
        )(codes, ends, queries, slots, rows, row_top, 1.0 / row_total, blocks_a, *blocks_b)

    sent = lax.ppermute(sums(0), "cand", [(i, i ^ 1) for i in range(2 * NY)])
    both = (sums(1) + sent).reshape(NY, QB, D)
    groups = [[2 * y + k for y in range(NY)] for k in range(2)]
    parts = lax.all_to_all(both, "cand", split_axis=0, concat_axis=0, axis_index_groups=groups, tiled=True)
    return (query_loss, jnp.sum(parts, axis=0))


def solution(mesh):
    in_specs = (P("corpus", None), P("corpus", None), P("corpus", "cand"), P("corpus"), P("corpus"))
    out_specs = (P("corpus"), P(("corpus", "cand"), None))
    return jax.shard_map(
        on_device, mesh=mesh, in_specs=in_specs, out_specs=out_specs, check_vma=False
    )
```

```python
import jax
import jax.numpy as jnp
from jax import lax
from jax.experimental import pallas as pl
from jax.experimental.pallas import tpu as pltpu
from jax.sharding import PartitionSpec as P

D = 768
QB = 128
PB = 128
PBD = 8
NC = 32
QBD = 8
PAIRS = 2 * QBD * NC
NX = 4
NZ = 16
NY = 4
GROUP = 2
WIDE = 2
STEP = GROUP * WIDE
SLOTS = 4
SCALE = D ** (-0.5)
LOW = -1e30


def for_steps(codes, low, high, blocks, buf, sems, body):
    def start(g, _):
        slot = lax.rem(g, SLOTS)
        for u in range(STEP):
            pltpu.make_async_copy(
                blocks.at[(codes[g * STEP + u] >> 6) & 31],
                buf.at[slot, pl.ds(u * PB, PB)],
                sems.at[slot],
            ).start()
        return 0

    lax.fori_loop(low, jnp.minimum(high, low + SLOTS), start, 0)

    def step(g, _):
        slot = lax.rem(g, SLOTS)
        pltpu.make_async_copy(buf.at[slot], buf.at[slot], sems.at[slot]).wait()
        groups = []
        for v in range(WIDE):
            code = [codes[g * STEP + v * GROUP + u] for u in range(GROUP)]
            block = buf[slot, v * GROUP * PB : (v + 1) * GROUP * PB]
            groups.append((block, code[0] >> 11, [(c & 63) - 1 for c in code]))
        body(groups)

        @pl.when(g + SLOTS < high)
        def _():
            start(g + SLOTS, 0)

        return 0

    lax.fori_loop(low, high, step, 0)


def scores_of(queries, block, e):
    q = queries[pl.ds(pl.multiple_of(e * QB, QB), QB), :]
    return lax.dot_general(
        block, q, (((1,), (1,)), ((), ())), preferred_element_type=jnp.float32
    ) * SCALE


def per_slot(slots, f):
    return jnp.concatenate([f(s) for s in slots], axis=0)


def positive_of(pos_slot, pos_row, e, slots):
    row = pl.ds(e, 1)
    here = lax.broadcasted_iota(jnp.int32, (PB, QB), 0) == pos_row[row, :]
    return per_slot(slots, lambda s: jnp.where(here & (pos_slot[row, :] == s), 1.0, 0.0))


def stats_kernel(
    codes, ends, queries, pos_slot, pos_row, blocks, out, buf, sems
):
    out[...] = jnp.zeros_like(out)
    out[0] = jnp.full((2 * QBD, QB), LOW, jnp.float32)

    def body(groups):
        scores = [scores_of(queries, block, e) for block, e, _ in groups]
        found = []
        for s, (_, e, slots) in zip(scores, groups):
            valid = per_slot(slots, lambda t: jnp.full((PB, QB), t, jnp.int32)) >= 0
            top = jnp.max(jnp.where(valid, s, LOW), axis=0, keepdims=True)
            terms = jnp.where(valid, jnp.exp(jnp.minimum(s - top, 0.0)), 0.0)
            hit = positive_of(pos_slot, pos_row, e, slots)
            found.append(
                (top, jnp.sum(terms, axis=0, keepdims=True), jnp.sum(hit * s, axis=0, keepdims=True))
            )
        for (top, total, hit), (_, e, _) in zip(found, groups):
            row = pl.ds(e, 1)
            old = out[0, row, :]
            new = jnp.maximum(old, top)
            out[0, row, :] = new
            out[1, row, :] = out[1, row, :] * jnp.exp(old - new) + total * jnp.exp(top - new)
            out[2, row, :] += hit

    for_steps(codes, 0, ends[1], blocks, buf, sems, body)


def sums_kernel(half):
    def kernel(
        codes, ends, queries, pos_slot, pos_row, row_top, row_scale, blocks, out, buf, sems
    ):
        out[...] = jnp.zeros_like(out)

        def body(groups):
            scores = [scores_of(queries, block, e) for block, e, _ in groups]
            weights = []
            for s, (_, e, slots) in zip(scores, groups):
                row = pl.ds(e, 1)
                valid = per_slot(slots, lambda t: jnp.full((PB, QB), t, jnp.int32)) >= 0
                w = jnp.exp(jnp.minimum(s - row_top[row, :], 0.0)) * row_scale[row, :]
                hit = positive_of(pos_slot, pos_row, e, slots)
                weights.append(
                    jnp.concatenate([jnp.where(valid, w, 0.0), hit], axis=1).astype(jnp.bfloat16)
                )
            terms = [
                lax.dot_general(
                    w, block, (((0,), (0,)), ((), ())), preferred_element_type=jnp.float32
                )
                for w, (block, _, _) in zip(weights, groups)
            ]
            for t, (_, e, _) in zip(terms, groups):
                rows = pl.ds(pl.multiple_of((e >> 1) * QB, QB), QB)
                out[rows, :] += t[:QB] - t[QB:]

        for_steps(codes, ends[0] if half else 0, ends[half], blocks, buf, sems, body)

    return kernel


VMEM = pl.BlockSpec(memory_space=pltpu.VMEM)
SMEM = pl.BlockSpec(memory_space=pltpu.SMEM)
HBM = pl.BlockSpec(memory_space=pl.ANY)
FETCH = [
    pltpu.VMEM((SLOTS, STEP * PB, D), jnp.bfloat16),
    pltpu.SemaphoreType.DMA((SLOTS,)),
]
PARAMS = pltpu.CompilerParams(vmem_limit_bytes=56 * 1024 * 1024)


def move_x(a, to):
    return lax.ppermute(
        a, "corpus", [(x * NZ + z, to(x) * NZ + z) for x in range(NX) for z in range(NZ)]
    )


def in_order(own, other, second):
    return jnp.where(second, jnp.stack([other, own]), jnp.stack([own, other]))


def team(z, m, cands):
    return [(x * NZ + z) * 2 * NY + c for x in (2 * m, 2 * m + 1) for c in cands]


TEAMS = [team(z, m, range(2 * NY)) for m in range(NX // 2) for z in range(NZ)]
CORES = [
    team(z, m, range(k, 2 * NY, 2)) for m in range(NX // 2) for z in range(NZ) for k in range(2)
]
LINES = [[x * NZ + z for z in range(NZ)] for x in range(NX)]


def on_device(queries, pool, candidate_block_table, pos_slot, pos_row):
    c = lax.axis_index("cand")
    core = c % 2
    x = lax.axis_index("corpus") // NZ
    second = x % 2 == 1

    mine = lax.dynamic_slice_in_dim(pool, c * PB, PB, 0)
    two = jnp.stack([mine, move_x(mine, lambda i: NX - 1 - i)])
    blocks = lax.all_gather(two, "corpus", axis=0, axis_index_groups=LINES, tiled=False)
    blocks = blocks.reshape(2 * NZ, PB, D)

    both_queries = in_order(queries, move_x(queries, lambda i: i ^ 1), second)
    both_queries = both_queries.reshape(2 * QBD * QB, D)
    positives = jnp.stack([pos_slot, pos_row]).reshape(2, QBD, QB)
    positives = in_order(positives, move_x(positives, lambda i: i ^ 1), second)
    slots, rows = positives[:, 0].reshape(2 * QBD, QB), positives[:, 1].reshape(2 * QBD, QB)
    table = lax.all_gather(candidate_block_table, "cand", axis=1, tiled=True)
    flat = in_order(table, move_x(table, lambda i: i ^ 1), second).reshape(PAIRS)

    number = jnp.arange(PAIRS, dtype=jnp.int32)
    owner = flat // PBD
    owner_x = owner // NZ
    held = (flat % PBD == c) & ((owner_x == x) | (owner_x == NX - 1 - x))
    code = number // NC * 2**11 + (owner % NZ * 2 + (owner_x != x)) * 2**6 + number % NC + 1
    by_e = held.reshape(2 * QBD, NC).astype(jnp.int32)
    padded = (jnp.sum(by_e, axis=1) + GROUP - 1) // GROUP * GROUP
    block = jnp.arange(2 * QBD)
    later = (block % 2 == core).astype(jnp.int32)
    turn = block + 2 * QBD * later
    in_class = (turn[None, :] < turn[:, None]) & (later[None, :] == later[:, None])
    sizes = jnp.stack([jnp.sum(padded * (1 - later)), jnp.sum(padded * later)])
    sizes = (sizes + STEP - 1) // STEP
    base = jnp.sum(jnp.where(in_class, padded[None, :], 0), axis=1) + later * sizes[0] * STEP
    before = number[:NC, None] > number[None, :NC]
    rank = jnp.sum(jnp.where(before[None], by_e[:, None, :], 0), axis=2)
    position = (base[:, None] + rank).reshape(PAIRS)
    place = held[None, :] & (position[None, :] == number[:, None])
    codes = jnp.sum(jnp.where(place, code[None, :], 0), axis=1)
    ends = jnp.stack([sizes[0], sizes[0] + sizes[1]])

    mine_stats = pl.pallas_call(
        stats_kernel,
        out_shape=jax.ShapeDtypeStruct((3, 2 * QBD, QB), jnp.float32),
        in_specs=[SMEM, SMEM, VMEM, VMEM, VMEM, HBM],
        out_specs=VMEM,
        scratch_shapes=FETCH,
        compiler_params=PARAMS,
        name="stats",
    )(codes, ends, both_queries, slots, rows, blocks)

    copies = jnp.broadcast_to(mine_stats, (4 * NY, *mine_stats.shape))
    stats = lax.all_to_all(
        copies, ("corpus", "cand"), split_axis=0, concat_axis=0, axis_index_groups=TEAMS, tiled=True
    )
    row_top = jnp.max(stats[:, 0], axis=0)
    row_total = jnp.sum(stats[:, 1] * jnp.exp(stats[:, 0] - row_top), axis=0)
    loss = row_top + jnp.log(row_total) - jnp.sum(stats[:, 2], axis=0)
    query_loss = jnp.where(second, loss[QBD:], loss[:QBD]).reshape(QBD * QB)

    def sums(half):
        return pl.pallas_call(
            sums_kernel(half),
            out_shape=jax.ShapeDtypeStruct((QBD * QB, D), jnp.float32),
            in_specs=[SMEM, SMEM, VMEM, VMEM, VMEM, VMEM, VMEM, HBM],
            out_specs=VMEM,
            scratch_shapes=FETCH,
            compiler_params=PARAMS,
            cost_estimate=pl.CostEstimate(flops=10**9, bytes_accessed=10**7, transcendentals=0),
            name="sums",
        )(codes, ends, both_queries, slots, rows, row_top, 1.0 / row_total, blocks)

    sent = lax.ppermute(sums(0), "cand", [(i, i ^ 1) for i in range(2 * NY)])
    both = (sums(1) + sent).reshape(2 * NY, QB, D)
    parts = lax.all_to_all(
        both, ("corpus", "cand"), split_axis=0, concat_axis=0, axis_index_groups=CORES, tiled=True
    )
    return (query_loss, jnp.sum(parts, axis=0))


def solution(mesh):
    in_specs = (P("corpus", None), P("corpus", None), P("corpus", "cand"), P("corpus"), P("corpus"))
    out_specs = (P("corpus"), P(("corpus", "cand"), None))
    return jax.shard_map(
        on_device, mesh=mesh, in_specs=in_specs, out_specs=out_specs, check_vma=False
    )
```

```python
import jax
import jax.numpy as jnp
from jax import lax
from jax.experimental import pallas as pl
from jax.experimental.pallas import tpu as pltpu
from jax.sharding import PartitionSpec as P

D = 768
QB = 128
PB = 128
PBD = 8
NC = 32
QBD = 8
PAIRS = 2 * QBD * NC
NX = 4
NZ = 16
NY = 4
GROUP = 2
WIDE = 2
STEP = GROUP * WIDE
SLOTS = 4
SCALE = D ** (-0.5)
LOW = -1e30


def for_steps(codes, low, high, blocks, buf, sems, body, more=()):
    def others(g, slot):
        return [pltpu.make_async_copy(ref.at[g], to.at[slot], s.at[slot]) for ref, to, s in more]

    def start(g, _):
        slot = lax.rem(g, SLOTS)
        for u in range(STEP):
            pltpu.make_async_copy(
                blocks.at[(codes[g * STEP + u] >> 6) & 31],
                buf.at[slot, pl.ds(u * PB, PB)],
                sems.at[slot],
            ).start()
        for c in others(g, slot):
            c.start()
        return 0

    lax.fori_loop(low, jnp.minimum(high, low + SLOTS), start, 0)

    def step(g, _):
        slot = lax.rem(g, SLOTS)
        pltpu.make_async_copy(buf.at[slot], buf.at[slot], sems.at[slot]).wait()
        for c in others(g, slot):
            c.wait()
        groups = []
        for v in range(WIDE):
            code = [codes[g * STEP + v * GROUP + u] for u in range(GROUP)]
            block = buf[slot, v * GROUP * PB : (v + 1) * GROUP * PB]
            groups.append((block, code[0] >> 11, [(c & 63) - 1 for c in code]))
        body(g, slot, groups)

        @pl.when(g + SLOTS < high)
        def _():
            start(g + SLOTS, 0)

        return 0

    lax.fori_loop(low, high, step, 0)


def scores_of(queries, block, e):
    q = queries[pl.ds(pl.multiple_of(e * QB, QB), QB), :]
    return lax.dot_general(
        block, q, (((1,), (1,)), ((), ())), preferred_element_type=jnp.float32
    ) * SCALE


def per_slot(slots, f):
    return jnp.concatenate([f(s) for s in slots], axis=0)


def positive_of(pos_slot, pos_row, e, slots):
    row = pl.ds(e, 1)
    here = lax.broadcasted_iota(jnp.int32, (PB, QB), 0) == pos_row[row, :]
    return per_slot(slots, lambda s: jnp.where(here & (pos_slot[row, :] == s), 1.0, 0.0))


def stats_kernel(
    codes, ends, queries, pos_slot, pos_row, blocks, out, tops, exps, buf, sems, kept, kept_sems
):
    out[...] = jnp.zeros_like(out)
    out[0] = jnp.full((2 * QBD, QB), LOW, jnp.float32)

    def keep(g):
        slot = lax.rem(g, 2)
        return pltpu.make_async_copy(kept.at[slot], exps.at[g], kept_sems.at[slot])

    def body(g, _, groups):
        scores = [scores_of(queries, block, e) for block, e, _ in groups]

        @pl.when(g >= 2)
        def _():
            keep(g - 2).wait()

        found = []
        for v, (s, (_, e, slots)) in enumerate(zip(scores, groups)):
            valid = per_slot(slots, lambda t: jnp.full((PB, QB), t, jnp.int32)) >= 0
            top = jnp.max(jnp.where(valid, s, LOW), axis=0, keepdims=True)
            terms = jnp.where(valid, jnp.exp(jnp.minimum(s - top, 0.0)), 0.0)
            kept[lax.rem(g, 2), v * GROUP * PB : (v + 1) * GROUP * PB] = terms
            hit = positive_of(pos_slot, pos_row, e, slots)
            found.append(
                (top, jnp.sum(terms, axis=0, keepdims=True), jnp.sum(hit * s, axis=0, keepdims=True))
            )
        keep(g).start()
        for v, ((top, total, hit), (_, e, _)) in enumerate(zip(found, groups)):
            tops[pl.ds(g * WIDE + v, 1), :] = top
            row = pl.ds(e, 1)
            old = out[0, row, :]
            new = jnp.maximum(old, top)
            out[0, row, :] = new
            out[1, row, :] = out[1, row, :] * jnp.exp(old - new) + total * jnp.exp(top - new)
            out[2, row, :] += hit

    high = ends[1]
    for_steps(codes, 0, high, blocks, buf, sems, body)
    for last in (2, 1):

        @pl.when(high >= last)
        def _():
            keep(high - last).wait()


def sums_kernel(half):
    def kernel(
        codes, ends, pos_slot, pos_row, row_top, row_scale, tops, exps, blocks, out, buf, sems, p_buf, p_sems
    ):
        out[...] = jnp.zeros_like(out)

        def body(g, slot, groups):
            weights = []
            for v, (_, e, slots) in enumerate(groups):
                row = pl.ds(e, 1)
                top = tops[pl.ds(g * WIDE + v, 1), :]
                scale = jnp.exp(jnp.minimum(top - row_top[row, :], 0.0)) * row_scale[row, :]
                w = p_buf[slot, v * GROUP * PB : (v + 1) * GROUP * PB] * scale
                hit = positive_of(pos_slot, pos_row, e, slots)
                weights.append(jnp.concatenate([w, hit], axis=1).astype(jnp.bfloat16))
            terms = [
                lax.dot_general(
                    w, block, (((0,), (0,)), ((), ())), preferred_element_type=jnp.float32
                )
                for w, (block, _, _) in zip(weights, groups)
            ]
            for t, (_, e, _) in zip(terms, groups):
                rows = pl.ds(pl.multiple_of((e >> 1) * QB, QB), QB)
                out[rows, :] += t[:QB] - t[QB:]

        low = ends[0] if half else 0
        for_steps(codes, low, ends[half], blocks, buf, sems, body, [(exps, p_buf, p_sems)])

    return kernel


VMEM = pl.BlockSpec(memory_space=pltpu.VMEM)
SMEM = pl.BlockSpec(memory_space=pltpu.SMEM)
HBM = pl.BlockSpec(memory_space=pltpu.HBM)
FETCH = [
    pltpu.VMEM((SLOTS, STEP * PB, D), jnp.bfloat16),
    pltpu.SemaphoreType.DMA((SLOTS,)),
]
KEEP = [pltpu.VMEM((2, STEP * PB, QB), jnp.float32), pltpu.SemaphoreType.DMA((2,))]
READ = [pltpu.VMEM((SLOTS, STEP * PB, QB), jnp.float32), pltpu.SemaphoreType.DMA((SLOTS,))]
PARAMS = pltpu.CompilerParams(vmem_limit_bytes=24 * 1024 * 1024)


def move_x(a, to):
    return lax.ppermute(
        a, "corpus", [(x * NZ + z, to(x) * NZ + z) for x in range(NX) for z in range(NZ)]
    )


def in_order(own, other, second):
    return jnp.where(second, jnp.stack([other, own]), jnp.stack([own, other]))


def team(z, m, cands):
    return [(x * NZ + z) * 2 * NY + c for x in (2 * m, 2 * m + 1) for c in cands]


TEAMS = [team(z, m, range(2 * NY)) for m in range(NX // 2) for z in range(NZ)]
CORES = [
    team(z, m, range(k, 2 * NY, 2)) for m in range(NX // 2) for z in range(NZ) for k in range(2)
]
LINES = [[x * NZ + z for z in range(NZ)] for x in range(NX)]


def on_device(queries, pool, candidate_block_table, pos_slot, pos_row):
    c = lax.axis_index("cand")
    core = c % 2
    x = lax.axis_index("corpus") // NZ
    second = x % 2 == 1

    mine = lax.dynamic_slice_in_dim(pool, c * PB, PB, 0)
    two = jnp.stack([mine, move_x(mine, lambda i: NX - 1 - i)])
    blocks = lax.all_gather(two, "corpus", axis=0, axis_index_groups=LINES, tiled=False)
    blocks = blocks.reshape(2 * NZ, PB, D)

    both_queries = in_order(queries, move_x(queries, lambda i: i ^ 1), second)
    both_queries = both_queries.reshape(2 * QBD * QB, D)
    positives = jnp.stack([pos_slot, pos_row]).reshape(2, QBD, QB)
    positives = in_order(positives, move_x(positives, lambda i: i ^ 1), second)
    slots, rows = positives[:, 0].reshape(2 * QBD, QB), positives[:, 1].reshape(2 * QBD, QB)
    table = lax.all_gather(candidate_block_table, "cand", axis=1, tiled=True)
    flat = in_order(table, move_x(table, lambda i: i ^ 1), second).reshape(PAIRS)

    number = jnp.arange(PAIRS, dtype=jnp.int32)
    owner = flat // PBD
    owner_x = owner // NZ
    held = (flat % PBD == c) & ((owner_x == x) | (owner_x == NX - 1 - x))
    code = number // NC * 2**11 + (owner % NZ * 2 + (owner_x != x)) * 2**6 + number % NC + 1
    by_e = held.reshape(2 * QBD, NC).astype(jnp.int32)
    padded = (jnp.sum(by_e, axis=1) + GROUP - 1) // GROUP * GROUP
    block = jnp.arange(2 * QBD)
    later = (block % 2 == core).astype(jnp.int32)
    turn = block + 2 * QBD * later
    in_class = (turn[None, :] < turn[:, None]) & (later[None, :] == later[:, None])
    sizes = jnp.stack([jnp.sum(padded * (1 - later)), jnp.sum(padded * later)])
    sizes = (sizes + STEP - 1) // STEP
    base = jnp.sum(jnp.where(in_class, padded[None, :], 0), axis=1) + later * sizes[0] * STEP
    before = number[:NC, None] > number[None, :NC]
    rank = jnp.sum(jnp.where(before[None], by_e[:, None, :], 0), axis=2)
    position = (base[:, None] + rank).reshape(PAIRS)
    place = held[None, :] & (position[None, :] == number[:, None])
    codes = jnp.sum(jnp.where(place, code[None, :], 0), axis=1)
    ends = jnp.stack([sizes[0], sizes[0] + sizes[1]])

    mine_stats, tops, exps = pl.pallas_call(
        stats_kernel,
        out_shape=(
            jax.ShapeDtypeStruct((3, 2 * QBD, QB), jnp.float32),
            jax.ShapeDtypeStruct((PAIRS // GROUP, QB), jnp.float32),
            jax.ShapeDtypeStruct((PAIRS // STEP, STEP * PB, QB), jnp.float32),
        ),
        in_specs=[SMEM, SMEM, VMEM, VMEM, VMEM, HBM],
        out_specs=(VMEM, VMEM, HBM),
        scratch_shapes=FETCH + KEEP,
        compiler_params=PARAMS,
        name="stats",
    )(codes, ends, both_queries, slots, rows, blocks)

    copies = jnp.broadcast_to(mine_stats, (4 * NY, *mine_stats.shape))
    stats = lax.all_to_all(
        copies, ("corpus", "cand"), split_axis=0, concat_axis=0, axis_index_groups=TEAMS, tiled=True
    )
    row_top = jnp.max(stats[:, 0], axis=0)
    row_total = jnp.sum(stats[:, 1] * jnp.exp(stats[:, 0] - row_top), axis=0)
    loss = row_top + jnp.log(row_total) - jnp.sum(stats[:, 2], axis=0)
    query_loss = jnp.where(second, loss[QBD:], loss[:QBD]).reshape(QBD * QB)

    def sums(half):
        return pl.pallas_call(
            sums_kernel(half),
            out_shape=jax.ShapeDtypeStruct((QBD * QB, D), jnp.float32),
            in_specs=[SMEM, SMEM, VMEM, VMEM, VMEM, VMEM, VMEM, HBM, HBM],
            out_specs=VMEM,
            scratch_shapes=FETCH + READ,
            compiler_params=PARAMS,
            cost_estimate=pl.CostEstimate(flops=10**9, bytes_accessed=10**7, transcendentals=0),
            name="sums",
        )(codes, ends, slots, rows, row_top, 1.0 / row_total, tops, exps, blocks)

    sent = lax.ppermute(sums(0), "cand", [(i, i ^ 1) for i in range(2 * NY)])
    both = (sums(1) + sent).reshape(2 * NY, QB, D)
    parts = lax.all_to_all(
        both, ("corpus", "cand"), split_axis=0, concat_axis=0, axis_index_groups=CORES, tiled=True
    )
    return (query_loss, jnp.sum(parts, axis=0))


def solution(mesh):
    in_specs = (P("corpus", None), P("corpus", None), P("corpus", "cand"), P("corpus"), P("corpus"))
    out_specs = (P("corpus"), P(("corpus", "cand"), None))
    return jax.shard_map(
        on_device, mesh=mesh, in_specs=in_specs, out_specs=out_specs, check_vma=False
    )
```

```python
import jax
import jax.numpy as jnp
from jax import lax
from jax.experimental import pallas as pl
from jax.experimental.pallas import tpu as pltpu
from jax.sharding import PartitionSpec as P

D = 768
QB = 128
PB = 128
PBD = 8
NC = 32
QBD = 8
PAIRS = 2 * QBD * NC
NX = 4
NZ = 16
NY = 4
GROUP = 2
WIDE = 2
STEP = GROUP * WIDE
SLOTS = 4
SCALE = D ** (-0.5)
LOW = -1e30


def for_steps(codes, low, high, blocks, buf, sems, body, more=()):
    def others(g, slot):
        return [pltpu.make_async_copy(ref.at[g], to.at[slot], s.at[slot]) for ref, to, s in more]

    def start(g, _):
        slot = lax.rem(g, SLOTS)
        for u in range(STEP):
            pltpu.make_async_copy(
                blocks.at[(codes[g * STEP + u] >> 6) & 31],
                buf.at[slot, pl.ds(u * PB, PB)],
                sems.at[slot],
            ).start()
        for c in others(g, slot):
            c.start()
        return 0

    lax.fori_loop(low, jnp.minimum(high, low + SLOTS), start, 0)

    def step(g, _):
        slot = lax.rem(g, SLOTS)
        pltpu.make_async_copy(buf.at[slot], buf.at[slot], sems.at[slot]).wait()
        for c in others(g, slot):
            c.wait()
        groups = []
        for v in range(WIDE):
            code = [codes[g * STEP + v * GROUP + u] for u in range(GROUP)]
            block = buf[slot, v * GROUP * PB : (v + 1) * GROUP * PB]
            groups.append((block, code[0] >> 11, [(c & 63) - 1 for c in code]))
        body(g, slot, groups)

        @pl.when(g + SLOTS < high)
        def _():
            start(g + SLOTS, 0)

        return 0

    lax.fori_loop(low, high, step, 0)


def scores_of(queries, block, e):
    q = queries[pl.ds(pl.multiple_of(e * QB, QB), QB), :]
    return lax.dot_general(
        block, q, (((1,), (1,)), ((), ())), preferred_element_type=jnp.float32
    ) * SCALE


def per_slot(slots, f):
    return jnp.concatenate([f(s) for s in slots], axis=0)


def positive_of(pos_slot, pos_row, e, slots):
    row = pl.ds(e, 1)
    here = lax.broadcasted_iota(jnp.int32, (PB, QB), 0) == pos_row[row, :]
    return per_slot(slots, lambda s: jnp.where(here & (pos_slot[row, :] == s), 1.0, 0.0))


def stats_kernel(
    codes, ends, queries, pos_slot, pos_row, blocks, out, tops, exps, buf, sems, kept, kept_sems
):
    out[...] = jnp.zeros_like(out)
    out[0] = jnp.full((2 * QBD, QB), LOW, jnp.float32)

    def keep(g):
        slot = lax.rem(g, 2)
        return pltpu.make_async_copy(kept.at[slot], exps.at[g], kept_sems.at[slot])

    def body(g, _, groups):
        scores = [scores_of(queries, block, e) for block, e, _ in groups]

        @pl.when(g >= 2)
        def _():
            keep(g - 2).wait()

        found = []
        for v, (s, (_, e, slots)) in enumerate(zip(scores, groups)):
            valid = per_slot(slots, lambda t: jnp.full((PB, QB), t, jnp.int32)) >= 0
            top = jnp.max(jnp.where(valid, s, LOW), axis=0, keepdims=True)
            terms = jnp.where(valid, jnp.exp(jnp.minimum(s - top, 0.0)), 0.0)
            kept[lax.rem(g, 2), v * GROUP * PB : (v + 1) * GROUP * PB] = terms
            hit = positive_of(pos_slot, pos_row, e, slots)
            found.append(
                (top, jnp.sum(terms, axis=0, keepdims=True), jnp.sum(hit * s, axis=0, keepdims=True))
            )
        keep(g).start()
        for v, ((top, total, hit), (_, e, _)) in enumerate(zip(found, groups)):
            tops[pl.ds(g * WIDE + v, 1), :] = top
            row = pl.ds(e, 1)
            old = out[0, row, :]
            new = jnp.maximum(old, top)
            out[0, row, :] = new
            out[1, row, :] = out[1, row, :] * jnp.exp(old - new) + total * jnp.exp(top - new)
            out[2, row, :] += hit

    high = ends[1]
    for_steps(codes, 0, high, blocks, buf, sems, body)
    for last in (2, 1):

        @pl.when(high >= last)
        def _():
            keep(high - last).wait()


def sums_kernel(half):
    def kernel(
        codes, ends, pos_slot, pos_row, row_top, row_scale, tops, exps, blocks, out, buf, sems, p_buf, p_sems
    ):
        out[...] = jnp.zeros_like(out)

        def body(g, slot, groups):
            weights = []
            for v, (_, e, slots) in enumerate(groups):
                row = pl.ds(e, 1)
                top = tops[pl.ds(g * WIDE + v, 1), :]
                scale = jnp.exp(jnp.minimum(top - row_top[row, :], 0.0)) * row_scale[row, :]
                w = p_buf[slot, v * GROUP * PB : (v + 1) * GROUP * PB] * scale
                hit = positive_of(pos_slot, pos_row, e, slots)
                weights.append(jnp.concatenate([w, hit], axis=1).astype(jnp.bfloat16))
            terms = [
                lax.dot_general(
                    w, block, (((0,), (0,)), ((), ())), preferred_element_type=jnp.float32
                )
                for w, (block, _, _) in zip(weights, groups)
            ]
            for t, (_, e, _) in zip(terms, groups):
                rows = pl.ds(pl.multiple_of((e >> 1) * QB, QB), QB)
                out[rows, :] += t[:QB] - t[QB:]

        low = ends[0] if half else 0
        for_steps(codes, low, ends[half], blocks, buf, sems, body, [(exps, p_buf, p_sems)])

    return kernel


VMEM = pl.BlockSpec(memory_space=pltpu.VMEM)
SMEM = pl.BlockSpec(memory_space=pltpu.SMEM)
HBM = pl.BlockSpec(memory_space=pltpu.HBM)
FETCH = [
    pltpu.VMEM((SLOTS, STEP * PB, D), jnp.bfloat16),
    pltpu.SemaphoreType.DMA((SLOTS,)),
]
KEEP = [pltpu.VMEM((2, STEP * PB, QB), jnp.float32), pltpu.SemaphoreType.DMA((2,))]
READ = [pltpu.VMEM((SLOTS, STEP * PB, QB), jnp.float32), pltpu.SemaphoreType.DMA((SLOTS,))]
PARAMS = pltpu.CompilerParams(vmem_limit_bytes=56 * 1024 * 1024)


def move_x(a, to):
    return lax.ppermute(
        a, "corpus", [(x * NZ + z, to(x) * NZ + z) for x in range(NX) for z in range(NZ)]
    )


def in_order(own, other, second):
    return jnp.where(second, jnp.stack([other, own]), jnp.stack([own, other]))


def team(z, m, cands):
    return [(x * NZ + z) * 2 * NY + c for x in (2 * m, 2 * m + 1) for c in cands]


TEAMS = [team(z, m, range(2 * NY)) for m in range(NX // 2) for z in range(NZ)]
CORES = [
    team(z, m, range(k, 2 * NY, 2)) for m in range(NX // 2) for z in range(NZ) for k in range(2)
]
LINES = [[x * NZ + z for z in range(NZ)] for x in range(NX)]


def on_device(queries, pool, candidate_block_table, pos_slot, pos_row):
    c = lax.axis_index("cand")
    core = c % 2
    x = lax.axis_index("corpus") // NZ
    second = x % 2 == 1

    mine = lax.dynamic_slice_in_dim(pool, c * PB, PB, 0)
    two = jnp.stack([mine, move_x(mine, lambda i: NX - 1 - i)])
    blocks = lax.all_gather(two, "corpus", axis=0, axis_index_groups=LINES, tiled=False)
    blocks = blocks.reshape(2 * NZ, PB, D)

    both_queries = in_order(queries, move_x(queries, lambda i: i ^ 1), second)
    both_queries = both_queries.reshape(2 * QBD * QB, D)
    positives = jnp.stack([pos_slot, pos_row]).reshape(2, QBD, QB)
    positives = in_order(positives, move_x(positives, lambda i: i ^ 1), second)
    slots, rows = positives[:, 0].reshape(2 * QBD, QB), positives[:, 1].reshape(2 * QBD, QB)
    table = lax.all_gather(candidate_block_table, "cand", axis=1, tiled=True)
    flat = in_order(table, move_x(table, lambda i: i ^ 1), second).reshape(PAIRS)

    number = jnp.arange(PAIRS, dtype=jnp.int32)
    owner = flat // PBD
    owner_x = owner // NZ
    held = (flat % PBD == c) & ((owner_x == x) | (owner_x == NX - 1 - x))
    code = number // NC * 2**11 + (owner % NZ * 2 + (owner_x != x)) * 2**6 + number % NC + 1
    by_e = held.reshape(2 * QBD, NC).astype(jnp.int32)
    padded = (jnp.sum(by_e, axis=1) + GROUP - 1) // GROUP * GROUP
    block = jnp.arange(2 * QBD)
    later = (block % 2 == core).astype(jnp.int32)
    turn = block + 2 * QBD * later
    in_class = (turn[None, :] < turn[:, None]) & (later[None, :] == later[:, None])
    sizes = jnp.stack([jnp.sum(padded * (1 - later)), jnp.sum(padded * later)])
    sizes = (sizes + STEP - 1) // STEP
    base = jnp.sum(jnp.where(in_class, padded[None, :], 0), axis=1) + later * sizes[0] * STEP
    before = number[:NC, None] > number[None, :NC]
    rank = jnp.sum(jnp.where(before[None], by_e[:, None, :], 0), axis=2)
    position = (base[:, None] + rank).reshape(PAIRS)
    place = held[None, :] & (position[None, :] == number[:, None])
    codes = jnp.sum(jnp.where(place, code[None, :], 0), axis=1)
    ends = jnp.stack([sizes[0], sizes[0] + sizes[1]])

    mine_stats, tops, exps = pl.pallas_call(
        stats_kernel,
        out_shape=(
            jax.ShapeDtypeStruct((3, 2 * QBD, QB), jnp.float32),
            jax.ShapeDtypeStruct((PAIRS // GROUP, QB), jnp.float32),
            jax.ShapeDtypeStruct((PAIRS // STEP, STEP * PB, QB), jnp.float32),
        ),
        in_specs=[SMEM, SMEM, VMEM, VMEM, VMEM, HBM],
        out_specs=(VMEM, VMEM, HBM),
        scratch_shapes=FETCH + KEEP,
        compiler_params=PARAMS,
        name="stats",
    )(codes, ends, both_queries, slots, rows, blocks)

    copies = jnp.broadcast_to(mine_stats, (4 * NY, *mine_stats.shape))
    stats = lax.all_to_all(
        copies, ("corpus", "cand"), split_axis=0, concat_axis=0, axis_index_groups=TEAMS, tiled=True
    )
    row_top = jnp.max(stats[:, 0], axis=0)
    row_total = jnp.sum(stats[:, 1] * jnp.exp(stats[:, 0] - row_top), axis=0)
    loss = row_top + jnp.log(row_total) - jnp.sum(stats[:, 2], axis=0)
    query_loss = jnp.where(second, loss[QBD:], loss[:QBD]).reshape(QBD * QB)

    def sums(half):
        return pl.pallas_call(
            sums_kernel(half),
            out_shape=jax.ShapeDtypeStruct((QBD * QB, D), jnp.float32),
            in_specs=[SMEM, SMEM, VMEM, VMEM, VMEM, VMEM, VMEM, HBM, HBM],
            out_specs=VMEM,
            scratch_shapes=FETCH + READ,
            compiler_params=PARAMS,
            cost_estimate=pl.CostEstimate(flops=10**9, bytes_accessed=10**7, transcendentals=0),
            name="sums",
        )(codes, ends, slots, rows, row_top, 1.0 / row_total, tops, exps, blocks)

    sent = lax.ppermute(sums(0), "cand", [(i, i ^ 1) for i in range(2 * NY)])
    both = (sums(1) + sent).reshape(2 * NY, QB, D)
    parts = lax.all_to_all(
        both, ("corpus", "cand"), split_axis=0, concat_axis=0, axis_index_groups=CORES, tiled=True
    )
    return (query_loss, jnp.sum(parts, axis=0))


def solution(mesh):
    in_specs = (P("corpus", None), P("corpus", None), P("corpus", "cand"), P("corpus"), P("corpus"))
    out_specs = (P("corpus"), P(("corpus", "cand"), None))
    return jax.shard_map(
        on_device, mesh=mesh, in_specs=in_specs, out_specs=out_specs, check_vma=False
    )
```

```python
import jax
import jax.numpy as jnp
from jax import lax
from jax.experimental import pallas as pl
from jax.experimental.pallas import tpu as pltpu
from jax.sharding import PartitionSpec as P

D = 768
QB = 128
PB = 128
PBD = 8
NC = 32
QBD = 8
PAIRS = 2 * QBD * NC
NX = 4
NZ = 16
NY = 4
GROUP = 2
WIDE = 4
STEP = GROUP * WIDE
SLOTS = 3
SCALE = D ** (-0.5)
LOW = -1e30


def for_steps(codes, low, high, blocks, buf, sems, body, more=()):
    def others(g, slot):
        return [pltpu.make_async_copy(ref.at[g], to.at[slot], s.at[slot]) for ref, to, s in more]

    def start(g, _):
        slot = lax.rem(g, SLOTS)
        for u in range(STEP):
            pltpu.make_async_copy(
                blocks.at[(codes[g * STEP + u] >> 6) & 31],
                buf.at[slot, pl.ds(u * PB, PB)],
                sems.at[slot],
            ).start()
        for c in others(g, slot):
            c.start()
        return 0

    lax.fori_loop(low, jnp.minimum(high, low + SLOTS), start, 0)

    def step(g, _):
        slot = lax.rem(g, SLOTS)
        pltpu.make_async_copy(buf.at[slot], buf.at[slot], sems.at[slot]).wait()
        for c in others(g, slot):
            c.wait()
        groups = []
        for v in range(WIDE):
            code = [codes[g * STEP + v * GROUP + u] for u in range(GROUP)]
            block = buf[slot, v * GROUP * PB : (v + 1) * GROUP * PB]
            groups.append((block, code[0] >> 11, [(c & 63) - 1 for c in code]))
        body(g, slot, groups)

        @pl.when(g + SLOTS < high)
        def _():
            start(g + SLOTS, 0)

        return 0

    lax.fori_loop(low, high, step, 0)


def scores_of(queries, block, e):
    q = queries[pl.ds(pl.multiple_of(e * QB, QB), QB), :]
    return lax.dot_general(
        block, q, (((1,), (1,)), ((), ())), preferred_element_type=jnp.float32
    ) * SCALE


def per_slot(slots, f):
    return jnp.concatenate([f(s) for s in slots], axis=0)


def positive_of(pos_slot, pos_row, e, slots):
    row = pl.ds(e, 1)
    here = lax.broadcasted_iota(jnp.int32, (PB, QB), 0) == pos_row[row, :]
    return per_slot(slots, lambda s: jnp.where(here & (pos_slot[row, :] == s), 1.0, 0.0))


def stats_kernel(
    codes, ends, queries, pos_slot, pos_row, blocks, out, tops, exps, buf, sems, kept, kept_sems
):
    out[...] = jnp.zeros_like(out)
    out[0] = jnp.full((2 * QBD, QB), LOW, jnp.float32)

    def keep(g):
        slot = lax.rem(g, 2)
        return pltpu.make_async_copy(kept.at[slot], exps.at[g], kept_sems.at[slot])

    def body(g, _, groups):
        scores = [scores_of(queries, block, e) for block, e, _ in groups]

        @pl.when(g >= 2)
        def _():
            keep(g - 2).wait()

        found = []
        for v, (s, (_, e, slots)) in enumerate(zip(scores, groups)):
            valid = per_slot(slots, lambda t: jnp.full((PB, QB), t, jnp.int32)) >= 0
            top = jnp.max(jnp.where(valid, s, LOW), axis=0, keepdims=True)
            terms = jnp.where(valid, jnp.exp(jnp.minimum(s - top, 0.0)), 0.0)
            kept[lax.rem(g, 2), v * GROUP * PB : (v + 1) * GROUP * PB] = terms
            hit = positive_of(pos_slot, pos_row, e, slots)
            found.append(
                (top, jnp.sum(terms, axis=0, keepdims=True), jnp.sum(hit * s, axis=0, keepdims=True))
            )
        keep(g).start()
        for v, ((top, total, hit), (_, e, _)) in enumerate(zip(found, groups)):
            tops[pl.ds(g * WIDE + v, 1), :] = top
            row = pl.ds(e, 1)
            old = out[0, row, :]
            new = jnp.maximum(old, top)
            out[0, row, :] = new
            out[1, row, :] = out[1, row, :] * jnp.exp(old - new) + total * jnp.exp(top - new)
            out[2, row, :] += hit

    high = ends[1]
    for_steps(codes, 0, high, blocks, buf, sems, body)
    for last in (2, 1):

        @pl.when(high >= last)
        def _():
            keep(high - last).wait()


def sums_kernel(half):
    def kernel(
        codes, ends, pos_slot, pos_row, row_top, row_scale, tops, exps, blocks, out, buf, sems, p_buf, p_sems
    ):
        out[...] = jnp.zeros_like(out)

        def body(g, slot, groups):
            weights = []
            for v, (_, e, slots) in enumerate(groups):
                row = pl.ds(e, 1)
                top = tops[pl.ds(g * WIDE + v, 1), :]
                scale = jnp.exp(jnp.minimum(top - row_top[row, :], 0.0)) * row_scale[row, :]
                w = p_buf[slot, v * GROUP * PB : (v + 1) * GROUP * PB] * scale
                hit = positive_of(pos_slot, pos_row, e, slots)
                weights.append(jnp.concatenate([w, hit], axis=1).astype(jnp.bfloat16))
            terms = [
                lax.dot_general(
                    w, block, (((0,), (0,)), ((), ())), preferred_element_type=jnp.float32
                )
                for w, (block, _, _) in zip(weights, groups)
            ]
            for t, (_, e, _) in zip(terms, groups):
                rows = pl.ds(pl.multiple_of((e >> 1) * QB, QB), QB)
                out[rows, :] += t[:QB] - t[QB:]

        low = ends[0] if half else 0
        for_steps(codes, low, ends[half], blocks, buf, sems, body, [(exps, p_buf, p_sems)])

    return kernel


VMEM = pl.BlockSpec(memory_space=pltpu.VMEM)
SMEM = pl.BlockSpec(memory_space=pltpu.SMEM)
HBM = pl.BlockSpec(memory_space=pltpu.HBM)
FETCH = [
    pltpu.VMEM((SLOTS, STEP * PB, D), jnp.bfloat16),
    pltpu.SemaphoreType.DMA((SLOTS,)),
]
KEEP = [pltpu.VMEM((2, STEP * PB, QB), jnp.float32), pltpu.SemaphoreType.DMA((2,))]
READ = [pltpu.VMEM((SLOTS, STEP * PB, QB), jnp.float32), pltpu.SemaphoreType.DMA((SLOTS,))]
PARAMS = pltpu.CompilerParams(vmem_limit_bytes=56 * 1024 * 1024)


def move_x(a, to):
    return lax.ppermute(
        a, "corpus", [(x * NZ + z, to(x) * NZ + z) for x in range(NX) for z in range(NZ)]
    )


def in_order(own, other, second):
    return jnp.where(second, jnp.stack([other, own]), jnp.stack([own, other]))


def team(z, m, cands):
    return [(x * NZ + z) * 2 * NY + c for x in (2 * m, 2 * m + 1) for c in cands]


TEAMS = [team(z, m, range(2 * NY)) for m in range(NX // 2) for z in range(NZ)]
CORES = [
    team(z, m, range(k, 2 * NY, 2)) for m in range(NX // 2) for z in range(NZ) for k in range(2)
]
LINES = [[x * NZ + z for z in range(NZ)] for x in range(NX)]


def on_device(queries, pool, candidate_block_table, pos_slot, pos_row):
    c = lax.axis_index("cand")
    core = c % 2
    x = lax.axis_index("corpus") // NZ
    second = x % 2 == 1

    mine = lax.dynamic_slice_in_dim(pool, c * PB, PB, 0)
    two = jnp.stack([mine, move_x(mine, lambda i: NX - 1 - i)])
    blocks = lax.all_gather(two, "corpus", axis=0, axis_index_groups=LINES, tiled=False)
    blocks = blocks.reshape(2 * NZ, PB, D)

    both_queries = in_order(queries, move_x(queries, lambda i: i ^ 1), second)
    both_queries = both_queries.reshape(2 * QBD * QB, D)
    positives = jnp.stack([pos_slot, pos_row]).reshape(2, QBD, QB)
    positives = in_order(positives, move_x(positives, lambda i: i ^ 1), second)
    slots, rows = positives[:, 0].reshape(2 * QBD, QB), positives[:, 1].reshape(2 * QBD, QB)
    table = lax.all_gather(candidate_block_table, "cand", axis=1, tiled=True)
    flat = in_order(table, move_x(table, lambda i: i ^ 1), second).reshape(PAIRS)

    number = jnp.arange(PAIRS, dtype=jnp.int32)
    owner = flat // PBD
    owner_x = owner // NZ
    held = (flat % PBD == c) & ((owner_x == x) | (owner_x == NX - 1 - x))
    code = number // NC * 2**11 + (owner % NZ * 2 + (owner_x != x)) * 2**6 + number % NC + 1
    by_e = held.reshape(2 * QBD, NC).astype(jnp.int32)
    padded = (jnp.sum(by_e, axis=1) + GROUP - 1) // GROUP * GROUP
    block = jnp.arange(2 * QBD)
    later = (block % 2 == core).astype(jnp.int32)
    turn = block + 2 * QBD * later
    in_class = (turn[None, :] < turn[:, None]) & (later[None, :] == later[:, None])
    sizes = jnp.stack([jnp.sum(padded * (1 - later)), jnp.sum(padded * later)])
    sizes = (sizes + STEP - 1) // STEP
    base = jnp.sum(jnp.where(in_class, padded[None, :], 0), axis=1) + later * sizes[0] * STEP
    before = number[:NC, None] > number[None, :NC]
    rank = jnp.sum(jnp.where(before[None], by_e[:, None, :], 0), axis=2)
    position = (base[:, None] + rank).reshape(PAIRS)
    place = held[None, :] & (position[None, :] == number[:, None])
    codes = jnp.sum(jnp.where(place, code[None, :], 0), axis=1)
    ends = jnp.stack([sizes[0], sizes[0] + sizes[1]])

    mine_stats, tops, exps = pl.pallas_call(
        stats_kernel,
        out_shape=(
            jax.ShapeDtypeStruct((3, 2 * QBD, QB), jnp.float32),
            jax.ShapeDtypeStruct((PAIRS // GROUP, QB), jnp.float32),
            jax.ShapeDtypeStruct((PAIRS // STEP, STEP * PB, QB), jnp.float32),
        ),
        in_specs=[SMEM, SMEM, VMEM, VMEM, VMEM, HBM],
        out_specs=(VMEM, VMEM, HBM),
        scratch_shapes=FETCH + KEEP,
        compiler_params=PARAMS,
        name="stats",
    )(codes, ends, both_queries, slots, rows, blocks)

    copies = jnp.broadcast_to(mine_stats, (4 * NY, *mine_stats.shape))
    stats = lax.all_to_all(
        copies, ("corpus", "cand"), split_axis=0, concat_axis=0, axis_index_groups=TEAMS, tiled=True
    )
    row_top = jnp.max(stats[:, 0], axis=0)
    row_total = jnp.sum(stats[:, 1] * jnp.exp(stats[:, 0] - row_top), axis=0)
    loss = row_top + jnp.log(row_total) - jnp.sum(stats[:, 2], axis=0)
    query_loss = jnp.where(second, loss[QBD:], loss[:QBD]).reshape(QBD * QB)

    def sums(half):
        return pl.pallas_call(
            sums_kernel(half),
            out_shape=jax.ShapeDtypeStruct((QBD * QB, D), jnp.float32),
            in_specs=[SMEM, SMEM, VMEM, VMEM, VMEM, VMEM, VMEM, HBM, HBM],
            out_specs=VMEM,
            scratch_shapes=FETCH + READ,
            compiler_params=PARAMS,
            cost_estimate=pl.CostEstimate(flops=10**9, bytes_accessed=10**7, transcendentals=0),
            name="sums",
        )(codes, ends, slots, rows, row_top, 1.0 / row_total, tops, exps, blocks)

    sent = lax.ppermute(sums(0), "cand", [(i, i ^ 1) for i in range(2 * NY)])
    both = (sums(1) + sent).reshape(2 * NY, QB, D)
    parts = lax.all_to_all(
        both, ("corpus", "cand"), split_axis=0, concat_axis=0, axis_index_groups=CORES, tiled=True
    )
    return (query_loss, jnp.sum(parts, axis=0))


def solution(mesh):
    in_specs = (P("corpus", None), P("corpus", None), P("corpus", "cand"), P("corpus"), P("corpus"))
    out_specs = (P("corpus"), P(("corpus", "cand"), None))
    return jax.shard_map(
        on_device, mesh=mesh, in_specs=in_specs, out_specs=out_specs, check_vma=False
    )
```

```python
import jax
import jax.numpy as jnp
from jax import lax
from jax.experimental import pallas as pl
from jax.experimental.pallas import tpu as pltpu
from jax.sharding import PartitionSpec as P

D = 768
QB = 128
PB = 128
PBD = 8
NC = 32
QBD = 8
PAIRS = 2 * QBD * NC
NX = 4
NZ = 16
NY = 4
GROUP = 2
WIDE = 2
STEP = GROUP * WIDE
SLOTS = 4
SCALE = D ** (-0.5)
LOW = -1e30


def for_steps(codes, low, high, blocks, buf, sems, body, more=()):
    def others(g, slot):
        return [pltpu.make_async_copy(ref.at[g], to.at[slot], s.at[slot]) for ref, to, s in more]

    def start(g, _):
        slot = lax.rem(g, SLOTS)
        for u in range(STEP):
            pltpu.make_async_copy(
                blocks.at[(codes[g * STEP + u] >> 6) & 31],
                buf.at[slot, pl.ds(u * PB, PB)],
                sems.at[slot],
            ).start()
        for c in others(g, slot):
            c.start()
        return 0

    lax.fori_loop(low, jnp.minimum(high, low + SLOTS), start, 0)

    def step(g, _):
        slot = lax.rem(g, SLOTS)
        pltpu.make_async_copy(buf.at[slot], buf.at[slot], sems.at[slot]).wait()
        for c in others(g, slot):
            c.wait()
        groups = []
        for v in range(WIDE):
            code = [codes[g * STEP + v * GROUP + u] for u in range(GROUP)]
            block = buf[slot, v * GROUP * PB : (v + 1) * GROUP * PB]
            groups.append((block, code[0] >> 11, [(c & 63) - 1 for c in code]))
        body(g, slot, groups)

        @pl.when(g + SLOTS < high)
        def _():
            start(g + SLOTS, 0)

        return 0

    lax.fori_loop(low, high, step, 0)


def scores_of(queries, block, e):
    q = queries[pl.ds(pl.multiple_of(e * QB, QB), QB), :]
    return lax.dot_general(
        block, q, (((1,), (1,)), ((), ())), preferred_element_type=jnp.float32
    ) * SCALE


def per_slot(slots, f):
    return jnp.concatenate([f(s) for s in slots], axis=0)


def positive_of(pos_slot, pos_row, e, slots):
    row = pl.ds(e, 1)
    here = lax.broadcasted_iota(jnp.int32, (PB, QB), 0) == pos_row[row, :]
    return per_slot(slots, lambda s: jnp.where(here & (pos_slot[row, :] == s), 1.0, 0.0))


def stats_kernel(
    codes, ends, queries, pos_slot, pos_row, blocks, out, tops, exps, buf, sems, kept, kept_sems
):
    out[...] = jnp.zeros_like(out)
    out[0] = jnp.full((2 * QBD, QB), LOW, jnp.float32)

    def keep(g):
        slot = lax.rem(g, 2)
        return pltpu.make_async_copy(kept.at[slot], exps.at[g], kept_sems.at[slot])

    def body(g, _, groups):
        scores = [scores_of(queries, block, e) for block, e, _ in groups]

        @pl.when(g >= 2)
        def _():
            keep(g - 2).wait()

        found = []
        for v, (s, (_, e, slots)) in enumerate(zip(scores, groups)):
            valid = per_slot(slots, lambda t: jnp.full((PB, QB), t, jnp.int32)) >= 0
            top = jnp.max(jnp.where(valid, s, LOW), axis=0, keepdims=True)
            terms = jnp.where(valid, jnp.exp(jnp.minimum(s - top, 0.0)), 0.0)
            kept[lax.rem(g, 2), v * GROUP * PB : (v + 1) * GROUP * PB] = terms
            hit = positive_of(pos_slot, pos_row, e, slots)
            found.append(
                (top, jnp.sum(terms, axis=0, keepdims=True), jnp.sum(hit * s, axis=0, keepdims=True))
            )
        keep(g).start()
        for v, ((top, total, hit), (_, e, _)) in enumerate(zip(found, groups)):
            tops[pl.ds(g * WIDE + v, 1), :] = top
            row = pl.ds(e, 1)
            old = out[0, row, :]
            new = jnp.maximum(old, top)
            out[0, row, :] = new
            out[1, row, :] = out[1, row, :] * jnp.exp(old - new) + total * jnp.exp(top - new)
            out[2, row, :] += hit

    high = ends[3]
    for_steps(codes, 0, high, blocks, buf, sems, body)
    for last in (2, 1):

        @pl.when(high >= last)
        def _():
            keep(high - last).wait()


def sums_kernel(kind):
    def kernel(
        codes, ends, pos_slot, pos_row, row_top, row_scale, tops, exps, blocks, out, buf, sems, p_buf, p_sems
    ):
        out[...] = jnp.zeros_like(out)

        def body(g, slot, groups):
            weights = []
            for v, (_, e, slots) in enumerate(groups):
                row = pl.ds(e, 1)
                top = tops[pl.ds(g * WIDE + v, 1), :]
                scale = jnp.exp(jnp.minimum(top - row_top[row, :], 0.0)) * row_scale[row, :]
                w = p_buf[slot, v * GROUP * PB : (v + 1) * GROUP * PB] * scale
                hit = positive_of(pos_slot, pos_row, e, slots)
                weights.append(jnp.concatenate([w, hit], axis=1).astype(jnp.bfloat16))
            terms = [
                lax.dot_general(
                    w, block, (((0,), (0,)), ((), ())), preferred_element_type=jnp.float32
                )
                for w, (block, _, _) in zip(weights, groups)
            ]
            for t, (_, e, _) in zip(terms, groups):
                rows = pl.ds(pl.multiple_of((((e >> 1) - ends[NY]) & (NY - 1)) * QB, QB), QB)
                out[rows, :] += t[:QB] - t[QB:]

        low = ends[kind - 1] if kind else 0
        for_steps(codes, low, ends[kind], blocks, buf, sems, body, [(exps, p_buf, p_sems)])

    return kernel


VMEM = pl.BlockSpec(memory_space=pltpu.VMEM)
SMEM = pl.BlockSpec(memory_space=pltpu.SMEM)
HBM = pl.BlockSpec(memory_space=pltpu.HBM)
FETCH = [
    pltpu.VMEM((SLOTS, STEP * PB, D), jnp.bfloat16),
    pltpu.SemaphoreType.DMA((SLOTS,)),
]
KEEP = [pltpu.VMEM((2, STEP * PB, QB), jnp.float32), pltpu.SemaphoreType.DMA((2,))]
READ = [pltpu.VMEM((SLOTS, STEP * PB, QB), jnp.float32), pltpu.SemaphoreType.DMA((SLOTS,))]
PARAMS = pltpu.CompilerParams(vmem_limit_bytes=56 * 1024 * 1024)


def move_x(a, to):
    return lax.ppermute(
        a, "corpus", [(x * NZ + z, to(x) * NZ + z) for x in range(NX) for z in range(NZ)]
    )


def deliver(a, flip, dy):
    pairs = []
    for i in range(NX * NZ):
        for c in range(2 * NY):
            to = (i // NZ ^ flip) * NZ + i % NZ
            pairs.append((i * 2 * NY + c, to * 2 * NY + (c + 2 * dy) % (2 * NY)))
    return lax.ppermute(a, ("corpus", "cand"), pairs)


def in_order(own, other, second):
    return jnp.where(second, jnp.stack([other, own]), jnp.stack([own, other]))


def team(z, m, cands):
    return [(x * NZ + z) * 2 * NY + c for x in (2 * m, 2 * m + 1) for c in cands]


TEAMS = [team(z, m, range(2 * NY)) for m in range(NX // 2) for z in range(NZ)]
LINES = [[x * NZ + z for z in range(NZ)] for x in range(NX)]


def on_device(queries, pool, candidate_block_table, pos_slot, pos_row):
    c = lax.axis_index("cand")
    core = c % 2
    x = lax.axis_index("corpus") // NZ
    second = x % 2 == 1

    mine = lax.dynamic_slice_in_dim(pool, c * PB, PB, 0)
    two = jnp.stack([mine, move_x(mine, lambda i: NX - 1 - i)])
    blocks = lax.all_gather(two, "corpus", axis=0, axis_index_groups=LINES, tiled=False)
    blocks = blocks.reshape(2 * NZ, PB, D)

    both_queries = in_order(queries, move_x(queries, lambda i: i ^ 1), second)
    both_queries = both_queries.reshape(2 * QBD * QB, D)
    positives = jnp.stack([pos_slot, pos_row]).reshape(2, QBD, QB)
    positives = in_order(positives, move_x(positives, lambda i: i ^ 1), second)
    slots, rows = positives[:, 0].reshape(2 * QBD, QB), positives[:, 1].reshape(2 * QBD, QB)
    table = lax.all_gather(candidate_block_table, "cand", axis=1, tiled=True)
    flat = in_order(table, move_x(table, lambda i: i ^ 1), second).reshape(PAIRS)

    number = jnp.arange(PAIRS, dtype=jnp.int32)
    owner = flat // PBD
    owner_x = owner // NZ
    held = (flat % PBD == c) & ((owner_x == x) | (owner_x == NX - 1 - x))
    code = number // NC * 2**11 + (owner % NZ * 2 + (owner_x != x)) * 2**6 + number % NC + 1
    by_e = held.reshape(2 * QBD, NC).astype(jnp.int32)
    padded = (jnp.sum(by_e, axis=1) + GROUP - 1) // GROUP * GROUP
    block = jnp.arange(2 * QBD)
    kind = 2 * (block // QBD == x % 2) + (block % 2 == core)
    same = kind[None, :] == jnp.arange(4)[:, None]
    sizes = (jnp.sum(jnp.where(same, padded, 0), axis=1) + STEP - 1) // STEP
    lower = jnp.arange(4)[None, :] <= jnp.arange(4)[:, None]
    ends = jnp.sum(jnp.where(lower, sizes[None, :], 0), axis=1)
    earlier = (block[None, :] < block[:, None]) & (kind[None, :] == kind[:, None])
    base = jnp.sum(jnp.where(earlier, padded[None, :], 0), axis=1)
    base = base + STEP * jnp.sum(jnp.where(same, (ends - sizes)[:, None], 0), axis=0)
    before = number[:NC, None] > number[None, :NC]
    rank = jnp.sum(jnp.where(before[None], by_e[:, None, :], 0), axis=2)
    position = (base[:, None] + rank).reshape(PAIRS)
    place = held[None, :] & (position[None, :] == number[:, None])
    codes = jnp.sum(jnp.where(place, code[None, :], 0), axis=1)
    ends = jnp.concatenate([ends, (c // 2)[None]]).astype(jnp.int32)

    mine_stats, tops, exps = pl.pallas_call(
        stats_kernel,
        out_shape=(
            jax.ShapeDtypeStruct((3, 2 * QBD, QB), jnp.float32),
            jax.ShapeDtypeStruct((PAIRS // GROUP, QB), jnp.float32),
            jax.ShapeDtypeStruct((PAIRS // STEP, STEP * PB, QB), jnp.float32),
        ),
        in_specs=[SMEM, SMEM, VMEM, VMEM, VMEM, HBM],
        out_specs=(VMEM, VMEM, HBM),
        scratch_shapes=FETCH + KEEP,
        compiler_params=PARAMS,
        name="stats",
    )(codes, ends, both_queries, slots, rows, blocks)

    copies = jnp.broadcast_to(mine_stats, (4 * NY, *mine_stats.shape))
    stats = lax.all_to_all(
        copies, ("corpus", "cand"), split_axis=0, concat_axis=0, axis_index_groups=TEAMS, tiled=True
    )
    row_top = jnp.max(stats[:, 0], axis=0)
    row_total = jnp.sum(stats[:, 1] * jnp.exp(stats[:, 0] - row_top), axis=0)
    loss = row_top + jnp.log(row_total) - jnp.sum(stats[:, 2], axis=0)
    query_loss = jnp.where(second, loss[QBD:], loss[:QBD]).reshape(QBD * QB)

    def sums(kind, tops):
        return pl.pallas_call(
            sums_kernel(kind),
            out_shape=jax.ShapeDtypeStruct((NY * QB, D), jnp.float32),
            in_specs=[SMEM, SMEM, VMEM, VMEM, VMEM, VMEM, VMEM, HBM, HBM],
            out_specs=VMEM,
            scratch_shapes=FETCH + READ,
            compiler_params=PARAMS,
            cost_estimate=pl.CostEstimate(flops=10**9, bytes_accessed=10**7, transcendentals=0),
            name="sums",
        )(codes, ends, slots, rows, row_top, 1.0 / row_total, tops, exps, blocks)

    def both_cores(kind, tops):
        sent = lax.ppermute(sums(kind, tops), "cand", [(i, i ^ 1) for i in range(2 * NY)])
        return (sums(kind + 1, tops) + sent).reshape(NY, QB, D)

    theirs = both_cores(0, tops)
    tops, theirs = lax.optimization_barrier((tops, theirs))
    parts = [deliver(theirs[d], 1, d) for d in (2, 1, 3, 0)]
    ours = both_cores(2, tops)
    parts += [deliver(ours[d], 0, d) for d in (2, 1, 3)]
    gradient = ours[0]
    for part in parts:
        gradient = gradient + part
    return (query_loss, gradient)


def solution(mesh):
    in_specs = (P("corpus", None), P("corpus", None), P("corpus", "cand"), P("corpus"), P("corpus"))
    out_specs = (P("corpus"), P(("corpus", "cand"), None))
    return jax.shard_map(
        on_device, mesh=mesh, in_specs=in_specs, out_specs=out_specs, check_vma=False
    )
```

```python
import jax
import jax.numpy as jnp
from jax import lax
from jax.experimental import pallas as pl
from jax.experimental.pallas import tpu as pltpu
from jax.sharding import PartitionSpec as P

D = 768
QB = 128
PB = 128
PBD = 8
NC = 32
QBD = 8
PAIRS = 2 * QBD * NC
NX = 4
NZ = 16
NY = 4
GROUP = 2
WIDE = 2
STEP = GROUP * WIDE
SLOTS = 4
SCALE = D ** (-0.5)
LOW = -1e30


def for_steps(codes, low, high, blocks, buf, sems, body, more=()):
    def others(g, slot):
        return [pltpu.make_async_copy(ref.at[g], to.at[slot], s.at[slot]) for ref, to, s in more]

    def start(g, _):
        slot = lax.rem(g, SLOTS)
        for u in range(STEP):
            pltpu.make_async_copy(
                blocks.at[(codes[g * STEP + u] >> 6) & 31],
                buf.at[slot, pl.ds(u * PB, PB)],
                sems.at[slot],
            ).start()
        for c in others(g, slot):
            c.start()
        return 0

    lax.fori_loop(low, jnp.minimum(high, low + SLOTS), start, 0)

    def step(g, _):
        slot = lax.rem(g, SLOTS)
        pltpu.make_async_copy(buf.at[slot], buf.at[slot], sems.at[slot]).wait()
        for c in others(g, slot):
            c.wait()
        groups = []
        for v in range(WIDE):
            code = [codes[g * STEP + v * GROUP + u] for u in range(GROUP)]
            block = buf[slot, v * GROUP * PB : (v + 1) * GROUP * PB]
            groups.append((block, code[0] >> 11, [(c & 63) - 1 for c in code]))
        body(g, slot, groups)

        @pl.when(g + SLOTS < high)
        def _():
            start(g + SLOTS, 0)

        return 0

    lax.fori_loop(low, high, step, 0)


def scores_of(queries, block, e):
    q = queries[pl.ds(pl.multiple_of(e * QB, QB), QB), :]
    return lax.dot_general(
        block, q, (((1,), (1,)), ((), ())), preferred_element_type=jnp.float32
    ) * SCALE


def per_slot(slots, f):
    return jnp.concatenate([f(s) for s in slots], axis=0)


def positive_of(pos_slot, pos_row, e, slots):
    row = pl.ds(e, 1)
    here = lax.broadcasted_iota(jnp.int32, (PB, QB), 0) == pos_row[row, :]
    return per_slot(slots, lambda s: jnp.where(here & (pos_slot[row, :] == s), 1.0, 0.0))


def stats_kernel(
    codes, ends, queries, pos_slot, pos_row, blocks, copies, tops, exps, buf, sems, kept, kept_sems
):
    out = copies.at[0]
    out[...] = jnp.zeros_like(out)
    out[0] = jnp.full((2 * QBD, QB), LOW, jnp.float32)

    def keep(g):
        slot = lax.rem(g, 2)
        return pltpu.make_async_copy(kept.at[slot], exps.at[g], kept_sems.at[slot])

    def body(g, _, groups):
        scores = [scores_of(queries, block, e) for block, e, _ in groups]

        @pl.when(g >= 2)
        def _():
            keep(g - 2).wait()

        found = []
        for v, (s, (_, e, slots)) in enumerate(zip(scores, groups)):
            valid = per_slot(slots, lambda t: jnp.full((PB, QB), t, jnp.int32)) >= 0
            top = jnp.max(jnp.where(valid, s, LOW), axis=0, keepdims=True)
            terms = jnp.where(valid, jnp.exp(jnp.minimum(s - top, 0.0)), 0.0)
            kept[lax.rem(g, 2), v * GROUP * PB : (v + 1) * GROUP * PB] = terms
            hit = positive_of(pos_slot, pos_row, e, slots)
            found.append(
                (top, jnp.sum(terms, axis=0, keepdims=True), jnp.sum(hit * s, axis=0, keepdims=True))
            )
        keep(g).start()
        for v, ((top, total, hit), (_, e, _)) in enumerate(zip(found, groups)):
            tops[pl.ds(g * WIDE + v, 1), :] = top
            row = pl.ds(e, 1)
            old = out[0, row, :]
            new = jnp.maximum(old, top)
            out[0, row, :] = new
            out[1, row, :] = out[1, row, :] * jnp.exp(old - new) + total * jnp.exp(top - new)
            out[2, row, :] += hit

    high = ends[1]
    for_steps(codes, 0, high, blocks, buf, sems, body)
    for last in (2, 1):

        @pl.when(high >= last)
        def _():
            keep(high - last).wait()

    for i in range(1, 4 * NY):
        copies[i] = out[...]


def sums_kernel(half):
    def kernel(
        codes, ends, pos_slot, pos_row, row_top, row_scale, tops, exps, blocks, out, buf, sems, p_buf, p_sems
    ):
        out[...] = jnp.zeros_like(out)

        def body(g, slot, groups):
            weights = []
            for v, (_, e, slots) in enumerate(groups):
                row = pl.ds(e, 1)
                top = tops[pl.ds(g * WIDE + v, 1), :]
                scale = jnp.exp(jnp.minimum(top - row_top[row, :], 0.0)) * row_scale[row, :]
                w = p_buf[slot, v * GROUP * PB : (v + 1) * GROUP * PB] * scale
                hit = positive_of(pos_slot, pos_row, e, slots)
                weights.append(jnp.concatenate([w, hit], axis=1).astype(jnp.bfloat16))
            terms = [
                lax.dot_general(
                    w, block, (((0,), (0,)), ((), ())), preferred_element_type=jnp.float32
                )
                for w, (block, _, _) in zip(weights, groups)
            ]
            for t, (_, e, _) in zip(terms, groups):
                rows = pl.ds(pl.multiple_of((e >> 1) * QB, QB), QB)
                out[rows, :] += t[:QB] - t[QB:]

        low = ends[0] if half else 0
        for_steps(codes, low, ends[half], blocks, buf, sems, body, [(exps, p_buf, p_sems)])

    return kernel


VMEM = pl.BlockSpec(memory_space=pltpu.VMEM)
SMEM = pl.BlockSpec(memory_space=pltpu.SMEM)
HBM = pl.BlockSpec(memory_space=pltpu.HBM)
FETCH = [
    pltpu.VMEM((SLOTS, STEP * PB, D), jnp.bfloat16),
    pltpu.SemaphoreType.DMA((SLOTS,)),
]
KEEP = [pltpu.VMEM((2, STEP * PB, QB), jnp.float32), pltpu.SemaphoreType.DMA((2,))]
READ = [pltpu.VMEM((SLOTS, STEP * PB, QB), jnp.float32), pltpu.SemaphoreType.DMA((SLOTS,))]
PARAMS = pltpu.CompilerParams(vmem_limit_bytes=56 * 1024 * 1024)


def move_x(a, to):
    return lax.ppermute(
        a, "corpus", [(x * NZ + z, to(x) * NZ + z) for x in range(NX) for z in range(NZ)]
    )


def in_order(own, other, second):
    return jnp.where(second, jnp.stack([other, own]), jnp.stack([own, other]))


def team(z, m, cands):
    return [(x * NZ + z) * 2 * NY + c for x in (2 * m, 2 * m + 1) for c in cands]


TEAMS = [team(z, m, range(2 * NY)) for m in range(NX // 2) for z in range(NZ)]
CORES = [
    team(z, m, range(k, 2 * NY, 2)) for m in range(NX // 2) for z in range(NZ) for k in range(2)
]
LINES = [[x * NZ + z for z in range(NZ)] for x in range(NX)]


def on_device(queries, pool, candidate_block_table, pos_slot, pos_row):
    c = lax.axis_index("cand")
    core = c % 2
    x = lax.axis_index("corpus") // NZ
    second = x % 2 == 1

    mine = lax.dynamic_slice_in_dim(pool, c * PB, PB, 0)
    two = jnp.stack([mine, move_x(mine, lambda i: NX - 1 - i)])
    blocks = lax.all_gather(two, "corpus", axis=0, axis_index_groups=LINES, tiled=False)
    blocks = blocks.reshape(2 * NZ, PB, D)

    both_queries = in_order(queries, move_x(queries, lambda i: i ^ 1), second)
    both_queries = both_queries.reshape(2 * QBD * QB, D)
    positives = jnp.stack([pos_slot, pos_row]).reshape(2, QBD, QB)
    positives = in_order(positives, move_x(positives, lambda i: i ^ 1), second)
    slots, rows = positives[:, 0].reshape(2 * QBD, QB), positives[:, 1].reshape(2 * QBD, QB)
    table = lax.all_gather(candidate_block_table, "cand", axis=1, tiled=True)
    flat = in_order(table, move_x(table, lambda i: i ^ 1), second).reshape(PAIRS)

    number = jnp.arange(PAIRS, dtype=jnp.int32)
    owner = flat // PBD
    owner_x = owner // NZ
    held = (flat % PBD == c) & ((owner_x == x) | (owner_x == NX - 1 - x))
    code = number // NC * 2**11 + (owner % NZ * 2 + (owner_x != x)) * 2**6 + number % NC + 1
    by_e = held.reshape(2 * QBD, NC).astype(jnp.int32)
    padded = (jnp.sum(by_e, axis=1) + GROUP - 1) // GROUP * GROUP
    block = jnp.arange(2 * QBD)
    later = (block % 2 == core).astype(jnp.int32)
    turn = block + 2 * QBD * later
    in_class = (turn[None, :] < turn[:, None]) & (later[None, :] == later[:, None])
    sizes = jnp.stack([jnp.sum(padded * (1 - later)), jnp.sum(padded * later)])
    sizes = (sizes + STEP - 1) // STEP
    base = jnp.sum(jnp.where(in_class, padded[None, :], 0), axis=1) + later * sizes[0] * STEP
    before = number[:NC, None] > number[None, :NC]
    rank = jnp.sum(jnp.where(before[None], by_e[:, None, :], 0), axis=2)
    position = (base[:, None] + rank).reshape(PAIRS)
    place = held[None, :] & (position[None, :] == number[:, None])
    codes = jnp.sum(jnp.where(place, code[None, :], 0), axis=1)
    ends = jnp.stack([sizes[0], sizes[0] + sizes[1]])

    mine_stats, tops, exps = pl.pallas_call(
        stats_kernel,
        out_shape=(
            jax.ShapeDtypeStruct((4 * NY, 3, 2 * QBD, QB), jnp.float32),
            jax.ShapeDtypeStruct((PAIRS // GROUP, QB), jnp.float32),
            jax.ShapeDtypeStruct((PAIRS // STEP, STEP * PB, QB), jnp.float32),
        ),
        in_specs=[SMEM, SMEM, VMEM, VMEM, VMEM, HBM],
        out_specs=(VMEM, VMEM, HBM),
        scratch_shapes=FETCH + KEEP,
        compiler_params=PARAMS,
        name="stats",
    )(codes, ends, both_queries, slots, rows, blocks)

    stats = lax.all_to_all(
        mine_stats, ("corpus", "cand"), split_axis=0, concat_axis=0, axis_index_groups=TEAMS, tiled=True
    )
    row_top = jnp.max(stats[:, 0], axis=0)
    row_total = jnp.sum(stats[:, 1] * jnp.exp(stats[:, 0] - row_top), axis=0)
    loss = row_top + jnp.log(row_total) - jnp.sum(stats[:, 2], axis=0)
    query_loss = jnp.where(second, loss[QBD:], loss[:QBD]).reshape(QBD * QB)

    def sums(half):
        return pl.pallas_call(
            sums_kernel(half),
            out_shape=jax.ShapeDtypeStruct((QBD * QB, D), jnp.float32),
            in_specs=[SMEM, SMEM, VMEM, VMEM, VMEM, VMEM, VMEM, HBM, HBM],
            out_specs=VMEM,
            scratch_shapes=FETCH + READ,
            compiler_params=PARAMS,
            cost_estimate=pl.CostEstimate(flops=10**9, bytes_accessed=10**7, transcendentals=0),
            name="sums",
        )(codes, ends, slots, rows, row_top, 1.0 / row_total, tops, exps, blocks)

    sent = lax.ppermute(sums(0), "cand", [(i, i ^ 1) for i in range(2 * NY)])
    both = (sums(1) + sent).reshape(2 * NY, QB, D)
    parts = lax.all_to_all(
        both, ("corpus", "cand"), split_axis=0, concat_axis=0, axis_index_groups=CORES, tiled=True
    )
    gradient = parts[0]
    for i in range(1, 2 * NY):
        gradient = gradient + parts[i]
    return (query_loss, gradient)


def solution(mesh):
    in_specs = (P("corpus", None), P("corpus", None), P("corpus", "cand"), P("corpus"), P("corpus"))
    out_specs = (P("corpus"), P(("corpus", "cand"), None))
    return jax.shard_map(
        on_device, mesh=mesh, in_specs=in_specs, out_specs=out_specs, check_vma=False
    )
```

```python
import jax
import jax.numpy as jnp
from jax import lax
from jax.experimental import pallas as pl
from jax.experimental.pallas import tpu as pltpu
from jax.sharding import PartitionSpec as P

D = 768
QB = 128
PB = 128
PBD = 8
NC = 32
QBD = 8
PAIRS = 2 * QBD * NC
NX = 4
NZ = 16
NY = 4
GROUP = 1
WIDE = 4
STEP = GROUP * WIDE
SLOTS = 4
SCALE = D ** (-0.5)
LOW = -1e30


def for_steps(codes, low, high, blocks, buf, sems, body, more=()):
    def others(g, slot):
        return [pltpu.make_async_copy(ref.at[g], to.at[slot], s.at[slot]) for ref, to, s in more]

    def start(g, _):
        slot = lax.rem(g, SLOTS)
        for u in range(STEP):
            pltpu.make_async_copy(
                blocks.at[(codes[g * STEP + u] >> 6) & 31],
                buf.at[slot, pl.ds(u * PB, PB)],
                sems.at[slot],
            ).start()
        for c in others(g, slot):
            c.start()
        return 0

    lax.fori_loop(low, jnp.minimum(high, low + SLOTS), start, 0)

    def step(g, _):
        slot = lax.rem(g, SLOTS)
        pltpu.make_async_copy(buf.at[slot], buf.at[slot], sems.at[slot]).wait()
        for c in others(g, slot):
            c.wait()
        groups = []
        for v in range(WIDE):
            code = [codes[g * STEP + v * GROUP + u] for u in range(GROUP)]
            block = buf[slot, v * GROUP * PB : (v + 1) * GROUP * PB]
            groups.append((block, code[0] >> 11, [(c & 63) - 1 for c in code]))
        body(g, slot, groups)

        @pl.when(g + SLOTS < high)
        def _():
            start(g + SLOTS, 0)

        return 0

    lax.fori_loop(low, high, step, 0)


def scores_of(queries, block, e):
    q = queries[pl.ds(pl.multiple_of(e * QB, QB), QB), :]
    return lax.dot_general(
        block, q, (((1,), (1,)), ((), ())), preferred_element_type=jnp.float32
    ) * SCALE


def per_slot(slots, f):
    return jnp.concatenate([f(s) for s in slots], axis=0)


def positive_of(pos_slot, pos_row, e, slots):
    row = pl.ds(e, 1)
    here = lax.broadcasted_iota(jnp.int32, (PB, QB), 0) == pos_row[row, :]
    return per_slot(slots, lambda s: jnp.where(here & (pos_slot[row, :] == s), 1.0, 0.0))


def stats_kernel(
    codes, ends, queries, pos_slot, pos_row, blocks, copies, tops, exps, buf, sems, kept, kept_sems
):
    out = copies.at[0]
    out[...] = jnp.zeros_like(out)
    out[0] = jnp.full((2 * QBD, QB), LOW, jnp.float32)

    def keep(g):
        slot = lax.rem(g, 2)
        return pltpu.make_async_copy(kept.at[slot], exps.at[g], kept_sems.at[slot])

    def body(g, _, groups):
        scores = [scores_of(queries, block, e) for block, e, _ in groups]

        @pl.when(g >= 2)
        def _():
            keep(g - 2).wait()

        found = []
        for v, (s, (_, e, slots)) in enumerate(zip(scores, groups)):
            valid = per_slot(slots, lambda t: jnp.full((PB, QB), t, jnp.int32)) >= 0
            top = jnp.max(jnp.where(valid, s, LOW), axis=0, keepdims=True)
            terms = jnp.where(valid, jnp.exp(jnp.minimum(s - top, 0.0)), 0.0)
            kept[lax.rem(g, 2), v * GROUP * PB : (v + 1) * GROUP * PB] = terms
            hit = positive_of(pos_slot, pos_row, e, slots)
            found.append(
                (top, jnp.sum(terms, axis=0, keepdims=True), jnp.sum(hit * s, axis=0, keepdims=True))
            )
        keep(g).start()
        for v, ((top, total, hit), (_, e, _)) in enumerate(zip(found, groups)):
            tops[pl.ds(g * WIDE + v, 1), :] = top
            row = pl.ds(e, 1)
            old = out[0, row, :]
            new = jnp.maximum(old, top)
            out[0, row, :] = new
            out[1, row, :] = out[1, row, :] * jnp.exp(old - new) + total * jnp.exp(top - new)
            out[2, row, :] += hit

    high = ends[1]
    for_steps(codes, 0, high, blocks, buf, sems, body)
    for last in (2, 1):

        @pl.when(high >= last)
        def _():
            keep(high - last).wait()

    for i in range(1, 4 * NY):
        copies[i] = out[...]


def sums_kernel(half):
    def kernel(
        codes, ends, pos_slot, pos_row, row_top, row_scale, tops, exps, blocks, out, buf, sems, p_buf, p_sems
    ):
        out[...] = jnp.zeros_like(out)

        def body(g, slot, groups):
            weights = []
            for v, (_, e, slots) in enumerate(groups):
                row = pl.ds(e, 1)
                top = tops[pl.ds(g * WIDE + v, 1), :]
                scale = jnp.exp(jnp.minimum(top - row_top[row, :], 0.0)) * row_scale[row, :]
                w = p_buf[slot, v * GROUP * PB : (v + 1) * GROUP * PB] * scale
                hit = positive_of(pos_slot, pos_row, e, slots)
                weights.append(jnp.concatenate([w, hit], axis=1).astype(jnp.bfloat16))
            terms = [
                lax.dot_general(
                    w, block, (((0,), (0,)), ((), ())), preferred_element_type=jnp.float32
                )
                for w, (block, _, _) in zip(weights, groups)
            ]
            for t, (_, e, _) in zip(terms, groups):
                rows = pl.ds(pl.multiple_of((e >> 1) * QB, QB), QB)
                out[rows, :] += t[:QB] - t[QB:]

        low = ends[0] if half else 0
        for_steps(codes, low, ends[half], blocks, buf, sems, body, [(exps, p_buf, p_sems)])

    return kernel


VMEM = pl.BlockSpec(memory_space=pltpu.VMEM)
SMEM = pl.BlockSpec(memory_space=pltpu.SMEM)
HBM = pl.BlockSpec(memory_space=pltpu.HBM)
FETCH = [
    pltpu.VMEM((SLOTS, STEP * PB, D), jnp.bfloat16),
    pltpu.SemaphoreType.DMA((SLOTS,)),
]
KEEP = [pltpu.VMEM((2, STEP * PB, QB), jnp.float32), pltpu.SemaphoreType.DMA((2,))]
READ = [pltpu.VMEM((SLOTS, STEP * PB, QB), jnp.float32), pltpu.SemaphoreType.DMA((SLOTS,))]
PARAMS = pltpu.CompilerParams(vmem_limit_bytes=56 * 1024 * 1024)


def move_x(a, to):
    return lax.ppermute(
        a, "corpus", [(x * NZ + z, to(x) * NZ + z) for x in range(NX) for z in range(NZ)]
    )


def in_order(own, other, second):
    return jnp.where(second, jnp.stack([other, own]), jnp.stack([own, other]))


def team(z, m, cands):
    return [(x * NZ + z) * 2 * NY + c for x in (2 * m, 2 * m + 1) for c in cands]


TEAMS = [team(z, m, range(2 * NY)) for m in range(NX // 2) for z in range(NZ)]
CORES = [
    team(z, m, range(k, 2 * NY, 2)) for m in range(NX // 2) for z in range(NZ) for k in range(2)
]
LINES = [[x * NZ + z for z in range(NZ)] for x in range(NX)]


def on_device(queries, pool, candidate_block_table, pos_slot, pos_row):
    c = lax.axis_index("cand")
    core = c % 2
    x = lax.axis_index("corpus") // NZ
    second = x % 2 == 1

    mine = lax.dynamic_slice_in_dim(pool, c * PB, PB, 0)
    two = jnp.stack([mine, move_x(mine, lambda i: NX - 1 - i)])
    blocks = lax.all_gather(two, "corpus", axis=0, axis_index_groups=LINES, tiled=False)
    blocks = blocks.reshape(2 * NZ, PB, D)

    both_queries = in_order(queries, move_x(queries, lambda i: i ^ 1), second)
    both_queries = both_queries.reshape(2 * QBD * QB, D)
    positives = jnp.stack([pos_slot, pos_row]).reshape(2, QBD, QB)
    positives = in_order(positives, move_x(positives, lambda i: i ^ 1), second)
    slots, rows = positives[:, 0].reshape(2 * QBD, QB), positives[:, 1].reshape(2 * QBD, QB)
    table = lax.all_gather(candidate_block_table, "cand", axis=1, tiled=True)
    flat = in_order(table, move_x(table, lambda i: i ^ 1), second).reshape(PAIRS)

    number = jnp.arange(PAIRS, dtype=jnp.int32)
    owner = flat // PBD
    owner_x = owner // NZ
    held = (flat % PBD == c) & ((owner_x == x) | (owner_x == NX - 1 - x))
    code = number // NC * 2**11 + (owner % NZ * 2 + (owner_x != x)) * 2**6 + number % NC + 1
    by_e = held.reshape(2 * QBD, NC).astype(jnp.int32)
    padded = (jnp.sum(by_e, axis=1) + GROUP - 1) // GROUP * GROUP
    block = jnp.arange(2 * QBD)
    later = (block % 2 == core).astype(jnp.int32)
    turn = block + 2 * QBD * later
    in_class = (turn[None, :] < turn[:, None]) & (later[None, :] == later[:, None])
    sizes = jnp.stack([jnp.sum(padded * (1 - later)), jnp.sum(padded * later)])
    sizes = (sizes + STEP - 1) // STEP
    base = jnp.sum(jnp.where(in_class, padded[None, :], 0), axis=1) + later * sizes[0] * STEP
    before = number[:NC, None] > number[None, :NC]
    rank = jnp.sum(jnp.where(before[None], by_e[:, None, :], 0), axis=2)
    position = (base[:, None] + rank).reshape(PAIRS)
    place = held[None, :] & (position[None, :] == number[:, None])
    codes = jnp.sum(jnp.where(place, code[None, :], 0), axis=1)
    ends = jnp.stack([sizes[0], sizes[0] + sizes[1]])

    mine_stats, tops, exps = pl.pallas_call(
        stats_kernel,
        out_shape=(
            jax.ShapeDtypeStruct((4 * NY, 3, 2 * QBD, QB), jnp.float32),
            jax.ShapeDtypeStruct((PAIRS // GROUP, QB), jnp.float32),
            jax.ShapeDtypeStruct((PAIRS // STEP, STEP * PB, QB), jnp.float32),
        ),
        in_specs=[SMEM, SMEM, VMEM, VMEM, VMEM, HBM],
        out_specs=(VMEM, VMEM, HBM),
        scratch_shapes=FETCH + KEEP,
        compiler_params=PARAMS,
        name="stats",
    )(codes, ends, both_queries, slots, rows, blocks)

    stats = lax.all_to_all(
        mine_stats, ("corpus", "cand"), split_axis=0, concat_axis=0, axis_index_groups=TEAMS, tiled=True
    )
    row_top = jnp.max(stats[:, 0], axis=0)
    row_total = jnp.sum(stats[:, 1] * jnp.exp(stats[:, 0] - row_top), axis=0)
    loss = row_top + jnp.log(row_total) - jnp.sum(stats[:, 2], axis=0)
    query_loss = jnp.where(second, loss[QBD:], loss[:QBD]).reshape(QBD * QB)

    def sums(half):
        return pl.pallas_call(
            sums_kernel(half),
            out_shape=jax.ShapeDtypeStruct((QBD * QB, D), jnp.float32),
            in_specs=[SMEM, SMEM, VMEM, VMEM, VMEM, VMEM, VMEM, HBM, HBM],
            out_specs=VMEM,
            scratch_shapes=FETCH + READ,
            compiler_params=PARAMS,
            cost_estimate=pl.CostEstimate(flops=10**9, bytes_accessed=10**7, transcendentals=0),
            name="sums",
        )(codes, ends, slots, rows, row_top, 1.0 / row_total, tops, exps, blocks)

    sent = lax.ppermute(sums(0), "cand", [(i, i ^ 1) for i in range(2 * NY)])
    both = (sums(1) + sent).reshape(2 * NY, QB, D)
    parts = lax.all_to_all(
        both, ("corpus", "cand"), split_axis=0, concat_axis=0, axis_index_groups=CORES, tiled=True
    )
    gradient = parts[0]
    for i in range(1, 2 * NY):
        gradient = gradient + parts[i]
    return (query_loss, gradient)


def solution(mesh):
    in_specs = (P("corpus", None), P("corpus", None), P("corpus", "cand"), P("corpus"), P("corpus"))
    out_specs = (P("corpus"), P(("corpus", "cand"), None))
    return jax.shard_map(
        on_device, mesh=mesh, in_specs=in_specs, out_specs=out_specs, check_vma=False
    )
```

```python
import jax
import jax.numpy as jnp
from jax import lax
from jax.experimental import pallas as pl
from jax.experimental.pallas import tpu as pltpu
from jax.sharding import PartitionSpec as P

D = 768
QB = 128
PB = 128
PBD = 8
NC = 32
QBD = 8
PAIRS = 2 * QBD * NC
NX = 4
NZ = 16
NY = 4
GROUP = 2
WIDE = 2
STEP = GROUP * WIDE
SLOTS = 6
SCALE = D ** (-0.5)
LOW = -1e30


def for_steps(codes, low, high, blocks, buf, sems, body, more=()):
    def others(g, slot):
        return [pltpu.make_async_copy(ref.at[g], to.at[slot], s.at[slot]) for ref, to, s in more]

    def start(g, _):
        slot = lax.rem(g, SLOTS)
        for u in range(STEP):
            pltpu.make_async_copy(
                blocks.at[(codes[g * STEP + u] >> 6) & 31],
                buf.at[slot, pl.ds(u * PB, PB)],
                sems.at[slot],
            ).start()
        for c in others(g, slot):
            c.start()
        return 0

    lax.fori_loop(low, jnp.minimum(high, low + SLOTS), start, 0)

    def step(g, _):
        slot = lax.rem(g, SLOTS)
        pltpu.make_async_copy(buf.at[slot], buf.at[slot], sems.at[slot]).wait()
        for c in others(g, slot):
            c.wait()
        groups = []
        for v in range(WIDE):
            code = [codes[g * STEP + v * GROUP + u] for u in range(GROUP)]
            block = buf[slot, v * GROUP * PB : (v + 1) * GROUP * PB]
            groups.append((block, code[0] >> 11, [(c & 63) - 1 for c in code]))
        body(g, slot, groups)

        @pl.when(g + SLOTS < high)
        def _():
            start(g + SLOTS, 0)

        return 0

    lax.fori_loop(low, high, step, 0)


def scores_of(queries, block, e):
    q = queries[pl.ds(pl.multiple_of(e * QB, QB), QB), :]
    return lax.dot_general(
        block, q, (((1,), (1,)), ((), ())), preferred_element_type=jnp.float32
    ) * SCALE


def per_slot(slots, f):
    return jnp.concatenate([f(s) for s in slots], axis=0)


def positive_of(pos_slot, pos_row, e, slots):
    row = pl.ds(e, 1)
    here = lax.broadcasted_iota(jnp.int32, (PB, QB), 0) == pos_row[row, :]
    return per_slot(slots, lambda s: jnp.where(here & (pos_slot[row, :] == s), 1.0, 0.0))


def stats_kernel(
    codes, ends, queries, pos_slot, pos_row, blocks, copies, tops, exps, buf, sems, kept, kept_sems
):
    out = copies.at[0]
    out[...] = jnp.zeros_like(out)
    out[0] = jnp.full((2 * QBD, QB), LOW, jnp.float32)

    def keep(g):
        slot = lax.rem(g, 2)
        return pltpu.make_async_copy(kept.at[slot], exps.at[g], kept_sems.at[slot])

    def body(g, _, groups):
        scores = [scores_of(queries, block, e) for block, e, _ in groups]

        @pl.when(g >= 2)
        def _():
            keep(g - 2).wait()

        found = []
        for v, (s, (_, e, slots)) in enumerate(zip(scores, groups)):
            valid = per_slot(slots, lambda t: jnp.full((PB, QB), t, jnp.int32)) >= 0
            top = jnp.max(jnp.where(valid, s, LOW), axis=0, keepdims=True)
            terms = jnp.where(valid, jnp.exp(jnp.minimum(s - top, 0.0)), 0.0)
            kept[lax.rem(g, 2), v * GROUP * PB : (v + 1) * GROUP * PB] = terms
            hit = positive_of(pos_slot, pos_row, e, slots)
            found.append(
                (top, jnp.sum(terms, axis=0, keepdims=True), jnp.sum(hit * s, axis=0, keepdims=True))
            )
        keep(g).start()
        for v, ((top, total, hit), (_, e, _)) in enumerate(zip(found, groups)):
            tops[pl.ds(g * WIDE + v, 1), :] = top
            row = pl.ds(e, 1)
            old = out[0, row, :]
            new = jnp.maximum(old, top)
            out[0, row, :] = new
            out[1, row, :] = out[1, row, :] * jnp.exp(old - new) + total * jnp.exp(top - new)
            out[2, row, :] += hit

    high = ends[1]
    for_steps(codes, 0, high, blocks, buf, sems, body)
    for last in (2, 1):

        @pl.when(high >= last)
        def _():
            keep(high - last).wait()

    for i in range(1, 4 * NY):
        copies[i] = out[...]


def sums_kernel(half):
    def kernel(
        codes, ends, pos_slot, pos_row, row_top, row_scale, tops, exps, blocks, out, buf, sems, p_buf, p_sems
    ):
        out[...] = jnp.zeros_like(out)

        def body(g, slot, groups):
            weights = []
            for v, (_, e, slots) in enumerate(groups):
                row = pl.ds(e, 1)
                top = tops[pl.ds(g * WIDE + v, 1), :]
                scale = jnp.exp(jnp.minimum(top - row_top[row, :], 0.0)) * row_scale[row, :]
                w = p_buf[slot, v * GROUP * PB : (v + 1) * GROUP * PB] * scale
                hit = positive_of(pos_slot, pos_row, e, slots)
                weights.append(jnp.concatenate([w, hit], axis=1).astype(jnp.bfloat16))
            terms = [
                lax.dot_general(
                    w, block, (((0,), (0,)), ((), ())), preferred_element_type=jnp.float32
                )
                for w, (block, _, _) in zip(weights, groups)
            ]
            for t, (_, e, _) in zip(terms, groups):
                rows = pl.ds(pl.multiple_of((e >> 1) * QB, QB), QB)
                out[rows, :] += t[:QB] - t[QB:]

        low = ends[0] if half else 0
        for_steps(codes, low, ends[half], blocks, buf, sems, body, [(exps, p_buf, p_sems)])

    return kernel


VMEM = pl.BlockSpec(memory_space=pltpu.VMEM)
SMEM = pl.BlockSpec(memory_space=pltpu.SMEM)
HBM = pl.BlockSpec(memory_space=pltpu.HBM)
FETCH = [
    pltpu.VMEM((SLOTS, STEP * PB, D), jnp.bfloat16),
    pltpu.SemaphoreType.DMA((SLOTS,)),
]
KEEP = [pltpu.VMEM((2, STEP * PB, QB), jnp.float32), pltpu.SemaphoreType.DMA((2,))]
READ = [pltpu.VMEM((SLOTS, STEP * PB, QB), jnp.float32), pltpu.SemaphoreType.DMA((SLOTS,))]
PARAMS = pltpu.CompilerParams(vmem_limit_bytes=56 * 1024 * 1024)


def move_x(a, to):
    return lax.ppermute(
        a, "corpus", [(x * NZ + z, to(x) * NZ + z) for x in range(NX) for z in range(NZ)]
    )


def in_order(own, other, second):
    return jnp.where(second, jnp.stack([other, own]), jnp.stack([own, other]))


def team(z, m, cands):
    return [(x * NZ + z) * 2 * NY + c for x in (2 * m, 2 * m + 1) for c in cands]


TEAMS = [team(z, m, range(2 * NY)) for m in range(NX // 2) for z in range(NZ)]
CORES = [
    team(z, m, range(k, 2 * NY, 2)) for m in range(NX // 2) for z in range(NZ) for k in range(2)
]
LINES = [[x * NZ + z for z in range(NZ)] for x in range(NX)]


def on_device(queries, pool, candidate_block_table, pos_slot, pos_row):
    c = lax.axis_index("cand")
    core = c % 2
    x = lax.axis_index("corpus") // NZ
    second = x % 2 == 1

    mine = lax.dynamic_slice_in_dim(pool, c * PB, PB, 0)
    two = jnp.stack([mine, move_x(mine, lambda i: NX - 1 - i)])
    blocks = lax.all_gather(two, "corpus", axis=0, axis_index_groups=LINES, tiled=False)
    blocks = blocks.reshape(2 * NZ, PB, D)

    both_queries = in_order(queries, move_x(queries, lambda i: i ^ 1), second)
    both_queries = both_queries.reshape(2 * QBD * QB, D)
    positives = jnp.stack([pos_slot, pos_row]).reshape(2, QBD, QB)
    positives = in_order(positives, move_x(positives, lambda i: i ^ 1), second)
    slots, rows = positives[:, 0].reshape(2 * QBD, QB), positives[:, 1].reshape(2 * QBD, QB)
    table = lax.all_gather(candidate_block_table, "cand", axis=1, tiled=True)
    flat = in_order(table, move_x(table, lambda i: i ^ 1), second).reshape(PAIRS)

    number = jnp.arange(PAIRS, dtype=jnp.int32)
    owner = flat // PBD
    owner_x = owner // NZ
    held = (flat % PBD == c) & ((owner_x == x) | (owner_x == NX - 1 - x))
    code = number // NC * 2**11 + (owner % NZ * 2 + (owner_x != x)) * 2**6 + number % NC + 1
    by_e = held.reshape(2 * QBD, NC).astype(jnp.int32)
    padded = (jnp.sum(by_e, axis=1) + GROUP - 1) // GROUP * GROUP
    block = jnp.arange(2 * QBD)
    later = (block % 2 == core).astype(jnp.int32)
    turn = block + 2 * QBD * later
    in_class = (turn[None, :] < turn[:, None]) & (later[None, :] == later[:, None])
    sizes = jnp.stack([jnp.sum(padded * (1 - later)), jnp.sum(padded * later)])
    sizes = (sizes + STEP - 1) // STEP
    base = jnp.sum(jnp.where(in_class, padded[None, :], 0), axis=1) + later * sizes[0] * STEP
    before = number[:NC, None] > number[None, :NC]
    rank = jnp.sum(jnp.where(before[None], by_e[:, None, :], 0), axis=2)
    position = (base[:, None] + rank).reshape(PAIRS)
    place = held[None, :] & (position[None, :] == number[:, None])
    codes = jnp.sum(jnp.where(place, code[None, :], 0), axis=1)
    ends = jnp.stack([sizes[0], sizes[0] + sizes[1]])

    mine_stats, tops, exps = pl.pallas_call(
        stats_kernel,
        out_shape=(
            jax.ShapeDtypeStruct((4 * NY, 3, 2 * QBD, QB), jnp.float32),
            jax.ShapeDtypeStruct((PAIRS // GROUP, QB), jnp.float32),
            jax.ShapeDtypeStruct((PAIRS // STEP, STEP * PB, QB), jnp.float32),
        ),
        in_specs=[SMEM, SMEM, VMEM, VMEM, VMEM, HBM],
        out_specs=(VMEM, VMEM, HBM),
        scratch_shapes=FETCH + KEEP,
        compiler_params=PARAMS,
        name="stats",
    )(codes, ends, both_queries, slots, rows, blocks)

    stats = lax.all_to_all(
        mine_stats, ("corpus", "cand"), split_axis=0, concat_axis=0, axis_index_groups=TEAMS, tiled=True
    )
    row_top = jnp.max(stats[:, 0], axis=0)
    row_total = jnp.sum(stats[:, 1] * jnp.exp(stats[:, 0] - row_top), axis=0)
    loss = row_top + jnp.log(row_total) - jnp.sum(stats[:, 2], axis=0)
    query_loss = jnp.where(second, loss[QBD:], loss[:QBD]).reshape(QBD * QB)

    def sums(half):
        return pl.pallas_call(
            sums_kernel(half),
            out_shape=jax.ShapeDtypeStruct((QBD * QB, D), jnp.float32),
            in_specs=[SMEM, SMEM, VMEM, VMEM, VMEM, VMEM, VMEM, HBM, HBM],
            out_specs=VMEM,
            scratch_shapes=FETCH + READ,
            compiler_params=PARAMS,
            cost_estimate=pl.CostEstimate(flops=10**9, bytes_accessed=10**7, transcendentals=0),
            name="sums",
        )(codes, ends, slots, rows, row_top, 1.0 / row_total, tops, exps, blocks)

    sent = lax.ppermute(sums(0), "cand", [(i, i ^ 1) for i in range(2 * NY)])
    both = (sums(1) + sent).reshape(2 * NY, QB, D)
    parts = lax.all_to_all(
        both, ("corpus", "cand"), split_axis=0, concat_axis=0, axis_index_groups=CORES, tiled=True
    )
    gradient = parts[0]
    for i in range(1, 2 * NY):
        gradient = gradient + parts[i]
    return (query_loss, gradient)


def solution(mesh):
    in_specs = (P("corpus", None), P("corpus", None), P("corpus", "cand"), P("corpus"), P("corpus"))
    out_specs = (P("corpus"), P(("corpus", "cand"), None))
    return jax.shard_map(
        on_device, mesh=mesh, in_specs=in_specs, out_specs=out_specs, check_vma=False
    )
```
